512 devices in a mesh: rows: 128 (over x_hi, y, z), cols: 4 (over x_lo, core).
Axes of the slice: x: 4 (x_hi: 2, x_lo: 2; x = x_hi * 2 + x_lo), y: 8, z: 8, core: 2. Of those that a mesh axis runs over, the one named last changes fastest.
Arguments:
- trace_limbs: float32 [2, 33554432], P(None, ('cols', 'rows')), parts along dimension 1, may hold values from 0 to 1, as said below
- coset_shift: int32 [1], replicated, may hold values from 1 to 2013265920
Outputs:
- extension: float32 [2, 67108864], P(None, ('cols', 'rows')), parts along dimension 1
The draws below stay inside these ranges and needn't reach their ends.
There are 4 independent parts, one for each index of `cols`. The reference program is written for one: setup_inputs(seed, part) draws one part's arguments, and reference() takes and returns one part's arrays. A program takes and returns all parts, laid end to end along the dimension named above; an argument that names none is the same for every part. Nothing has to cross between parts.
Inputs may be any that keep to these rules, and one draw needn't show every extreme that they name: `trace_limbs`: every entry is a whole multiple of 2**-16, and the entries of the second limb row are below one half.
All inputs are finite; a program needn't handle non-finite values.
Results may differ from the reference program's by a relative error of at most 0.0003.
Values may be sent and summed in bfloat16 or wider, within the bound.
No kernel may reach another device: no remote copies, remote signals or barrier semaphores. Data moves between devices by JAX's collectives and lax.ppermute only.
A program may use at most 128 MiB of HBM per device.

```python
import jax
import jax.numpy as jnp

LEN_A = 2048
LEN_B = 4096


def draw_trace_limbs(key, part):
    key = jax.random.fold_in(key, 11)
    low_key, high_key = jax.random.split(key)
    low_part = jax.random.randint(low_key, (LEN_A * LEN_B,), 0, 65536)
    high_part = jax.random.randint(high_key, (LEN_A * LEN_B,), 0, 32768)
    return jnp.stack([low_part, high_part]).astype(jnp.float32) / 65536.0


def setup_inputs(seed: int = 0, part: int = 0) -> dict:
    streams_of = jax.random.split(jax.random.key(seed), 3)
    own_keys = jax.random.split(jax.random.fold_in(streams_of[2], part), 3)
    return {
        "trace_limbs": draw_trace_limbs(jax.random.fold_in(jax.random.fold_in(streams_of[2], part), 71), part),
        "coset_shift": jax.random.randint(streams_of[1], (1,), 1, 2013265921).astype(jnp.int32),
    }


MODULUS = 2013265921


def unity_root(length):
    return pow(pow(31, 15, MODULUS), (1 << 27) // length, MODULUS)


def reduce_product(small_factor, field_factor):
    estimate = jnp.floor(small_factor.astype(jnp.float32) * field_factor.astype(jnp.float32) * (1.0 / MODULUS) + 0.5)
    remainder = small_factor * field_factor - estimate.astype(jnp.int32) * MODULUS
    return jnp.where(remainder < 0, remainder + MODULUS, remainder)


def field_add(first_term, second_term):
    summed = first_term - MODULUS + second_term
    return jnp.where(summed < 0, summed + MODULUS, summed)


def field_sub(first_term, second_term):
    differ = first_term - second_term
    return jnp.where(differ < 0, differ + MODULUS, differ)


def field_mul(factor_one, factor_two):
    high_part = reduce_product(factor_one >> 16, factor_two)
    low_part = reduce_product(factor_one & 65535, factor_two)
    return field_add(reduce_product(jnp.int32(65536), high_part), low_part)


def const_powers(base_value, exponents, bit_count):
    result = jnp.ones_like(exponents)
    for bit_level in range(bit_count):
        factor = jnp.where(((exponents >> bit_level) & 1) == 1, jnp.int32(pow(base_value, 1 << bit_level, MODULUS)), jnp.int32(1))
        result = field_mul(result, factor)
    return result


def traced_powers(base_value, exponents, bit_count):
    result = jnp.ones_like(exponents)
    square = base_value
    for bit_level in range(bit_count):
        result = jnp.where(((exponents >> bit_level) & 1) == 1, field_mul(result, square), result)
        square = field_mul(square, square)
    return result


def power_table(base_value, length):
    low_count = min(64, length)
    low_part = const_powers(base_value, jnp.arange(low_count, dtype=jnp.int32), 6)
    high_count = length // low_count
    high_part = const_powers(pow(base_value, low_count, MODULUS), jnp.arange(high_count, dtype=jnp.int32), max(1, high_count.bit_length()))
    return field_mul(high_part[:, None], low_part[None, :]).reshape(length)


def transform(values, root_table):
    length = values.shape[-1]
    row_count = values.size // length
    state = values.reshape(row_count, length)
    leading = state.T.reshape(1, length * row_count)
    half_span = 1
    while half_span < length and half_span < 128:
        groups = length // (2 * half_span)
        halves = leading.reshape(half_span, 2, groups * row_count)
        even_part = halves[:, 0]
        odd_part = halves[:, 1]
        twiddles = root_table[::groups]
        product = field_mul(odd_part, twiddles[:, None])
        leading = jnp.stack([field_add(even_part, product), field_sub(even_part, product)], 0).reshape(2 * half_span, groups * row_count)
        half_span = half_span * 2
    state = leading.reshape(half_span, length // half_span, row_count).transpose(2, 1, 0).reshape(row_count, length)
    while half_span < length:
        groups = length // (2 * half_span)
        halves = state.reshape(row_count, 2, length // 2)
        even_part = halves[:, 0]
        odd_part = halves[:, 1]
        twiddles = jnp.tile(root_table[::groups], groups)
        product = field_mul(odd_part, twiddles[None, :])
        sum_part = field_add(even_part, product).reshape(row_count, groups, half_span)
        diff_part = field_sub(even_part, product).reshape(row_count, groups, half_span)
        state = jnp.stack([sum_part, diff_part], 2).reshape(row_count, length)
        half_span = half_span * 2
    return state.reshape(values.shape)


def from_limbs(trace_limbs):
    low_part = (trace_limbs[0] * 65536.0).astype(jnp.int32)
    high_part = (trace_limbs[1] * 65536.0).astype(jnp.int32)
    joined = high_part * 65536 + low_part
    return jnp.where(joined >= MODULUS, joined - MODULUS, joined)


def to_limbs(field_values):
    return jnp.stack([(field_values & 65535).astype(jnp.float32), (field_values >> 16).astype(jnp.float32)]) / 65536.0


def reference(trace_limbs, coset_shift):
    values = from_limbs(trace_limbs)
    trace_len = values.shape[0]
    back_root = pow(unity_root(trace_len), MODULUS - 2, MODULUS)
    coeffs = transform(values, power_table(back_root, trace_len // 2))
    inverse_len = pow(trace_len, MODULUS - 2, MODULUS)
    shift_base = coset_shift[0]
    low_powers = field_mul(traced_powers(shift_base, jnp.arange(64, dtype=jnp.int32), 6), jnp.int32(inverse_len))
    step_power = traced_powers(shift_base, jnp.array([64], dtype=jnp.int32), 7)[0]
    high_count = trace_len // 64
    high_powers = traced_powers(step_power, jnp.arange(high_count, dtype=jnp.int32), high_count.bit_length())
    weights = field_mul(high_powers[:, None], low_powers[None, :]).reshape(trace_len)
    shifted = jnp.concatenate([field_mul(coeffs, weights), jnp.zeros((trace_len,), jnp.int32)])
    extended = transform(shifted, power_table(unity_root(2 * trace_len), trace_len))
    return to_limbs(extended)
```

```python
import functools

import jax
import jax.numpy as jnp
import ml_dtypes
import numpy as np
from jax import lax
from jax.experimental import pallas as pl
from jax.experimental.pallas import tpu as pltpu
from jax.sharding import PartitionSpec as P

LEN_A = 2048
LEN_B = 4096
MODULUS = 2013265921
HALF = MODULUS // 2
SPLIT = 15
LIMBS = 4
BYTE_BIAS = -2139062144

TRACE_LEN = LEN_A * LEN_B
EXT_LEN = 2 * TRACE_LEN
GROUP = 128
SIDE = 256
LONG = 2 * SIDE
LOCAL = SIDE * SIDE
LANES = 128


def unity_root(length):
    return pow(pow(31, 15, MODULUS), (1 << 27) // length, MODULUS)


BACK_ROOT = pow(unity_root(TRACE_LEN), MODULUS - 2, MODULUS)
FWD_ROOT = unity_root(EXT_LEN)


def powers_of(base, exponents):
    exponents = np.asarray(exponents, dtype=np.int64)
    result = np.ones(exponents.shape, dtype=np.int64)
    square = base % MODULUS
    for bit in range(int(exponents.max(initial=0)).bit_length()):
        result = np.where(exponents >> bit & 1 == 1, mul_mod(result, square), result)
        square = square * square % MODULUS
    return result


def mul_mod(left, right):
    return left * right % MODULUS


def centered(values):
    values = values % MODULUS
    return np.where(values > HALF, values - MODULUS, values)


def both_halves(values):
    return np.stack([centered(values), centered(mul_mod(values, 1 << SPLIT))]).astype(np.int32)


def limbs_of(values):
    rest = centered(values)
    digits = []
    for _ in range(LIMBS):
        digit = (rest + 128) % 256 - 128
        digits.append(digit)
        rest = (rest - digit) // 256
    return np.stack(digits)


def limb_matrix(matrix):
    blocks = np.stack([limbs_of(mul_mod(matrix, 256**a)) for a in range(LIMBS)], axis=2)
    out_len, in_len = matrix.shape
    return np.ascontiguousarray(
        blocks.reshape(LIMBS * out_len, LIMBS * in_len).astype(ml_dtypes.bfloat16)
    )


def dft_matrix(root, out_len, in_len):
    return powers_of(root, np.arange(out_len)[:, None] * np.arange(in_len)[None, :])


SPLIT_OUT = 2
MATRIX_ROWS = 3 * LIMBS * SIDE
TABLE_ROWS = 4096
LINE_ROWS = 16
LINES_AT = 1024


def in_parts(matrix, count):
    rows, cols = matrix.shape
    parts = matrix.reshape(LIMBS, SPLIT_OUT, count // SPLIT_OUT, cols).transpose(1, 0, 2, 3)
    return parts.reshape(rows, cols)


@functools.cache
def tables():
    lines = np.arange(GROUP)
    side = np.arange(SIDE)
    long = np.arange(LONG)
    tile = np.arange(LOCAL // GROUP)
    root_side = unity_root(SIDE)
    back_side = pow(root_side, MODULUS - 2, MODULUS)
    root_group = unity_root(GROUP)
    back_group = pow(root_group, MODULUS - 2, MODULUS)
    back_local = pow(unity_root(LOCAL), MODULUS - 2, MODULUS)
    side_back = limb_matrix(dft_matrix(back_side, SIDE, SIDE))
    wide = LIMBS * SIDE
    matrices = np.zeros((MATRIX_ROWS, 2 * wide), ml_dtypes.bfloat16)
    matrices[:wide] = in_parts(limb_matrix(dft_matrix(unity_root(LONG), LONG, SIDE)), LONG).T
    matrices[wide : 2 * wide, :wide] = in_parts(side_back, SIDE)
    matrices[wide : 2 * wide, wide:] = limb_matrix(dft_matrix(root_side, SIDE, SIDE))
    small = LIMBS * GROUP
    matrices[2 * wide :, :small] = np.concatenate(
        [limb_matrix(dft_matrix(root, GROUP, GROUP)) for root in (back_group, root_group)]
    )

    powers = np.zeros((TABLE_ROWS, LONG), np.int32)
    powers[0:512] = both_halves(
        powers_of(unity_root(2 * LOCAL), side[:, None] * long[None, :])
    ).reshape(512, LONG)
    powers[512:768] = np.concatenate(
        both_halves(powers_of(back_local, side[:, None] * side[None, :])), axis=1
    )
    powers[768:1024] = both_halves(
        powers_of(BACK_ROOT, lines[:, None] * tile[None, :])
    ).reshape(256, LONG)
    own = np.zeros((GROUP, LINE_ROWS, LONG), np.int32)

    def place_pair(root, exponents, row, lane):
        pair = both_halves(powers_of(root, lines[:, None] * exponents[None, :]))
        own[:, row : row + 2, lane : lane + exponents.size] = pair.transpose(1, 0, 2)

    place_pair(FWD_ROOT, long, 0, 0)
    place_pair(FWD_ROOT, LONG * side, 8, 0)
    place_pair(BACK_ROOT, tile.size * lines, 8, SIDE)
    powers[LINES_AT : LINES_AT + GROUP * LINE_ROWS] = own.reshape(GROUP * LINE_ROWS, LONG)
    return matrices, powers


def times_modulus(count):
    return (count << 31) - (count << 27) + count


def toward_zero(value):
    return value.astype(jnp.int32)


def to_nearest(value):
    return jnp.floor(value + 0.5).astype(jnp.int32)


def paired_mul(value, plain, lifted, whole=toward_zero):
    high = value >> SPLIT
    low = value & ((1 << SPLIT) - 1)
    scale = np.float32(1.0 / MODULUS)
    estimate = high.astype(jnp.float32) * (lifted.astype(jnp.float32) * scale) + low.astype(
        jnp.float32
    ) * (plain.astype(jnp.float32) * scale)
    return high * lifted + low * plain - times_modulus(whole(estimate))


near_mul = functools.partial(paired_mul, whole=to_nearest)


def lift(value):
    once, twice = (int(centered(np.int64(1 << k * SPLIT))) for k in (1, 2))
    return near_mul(value, jnp.int32(once), jnp.int32(twice))


def digits(value, axis):
    biased = (value + jnp.int32(BYTE_BIAS)) ^ jnp.int32(BYTE_BIAS)
    parts = [(biased << (24 - 8 * k)) >> 24 for k in range(LIMBS - 1)] + [biased >> 24]
    return jnp.concatenate([part.astype(jnp.float32).astype(jnp.bfloat16) for part in parts], axis)


def combine(part0, part1, part2, part3):
    estimate = (
        part3 * np.float32(2.0**24 / MODULUS)
        + part2 * np.float32(2.0**16 / MODULUS)
        + part1 * np.float32(2.0**8 / MODULUS)
    )
    whole = [part.astype(jnp.int32) for part in (part0, part1, part2, part3)]
    total = whole[0] + (whole[1] << 8) + (whole[2] << 16) + (whole[3] << 24)
    return total - times_modulus(toward_zero(estimate))


def dot(left, right):
    return jnp.dot(left, right, preferred_element_type=jnp.float32)


def from_rows(result, count):
    return combine(*(result[k * count : (k + 1) * count] for k in range(LIMBS)))


def from_cols(result, count):
    return combine(*(result[:, k * count : (k + 1) * count] for k in range(LIMBS)))


def load(sources, targets, sems):
    copies = [
        pltpu.make_async_copy(source, target, sems.at[k])
        for k, (source, target) in enumerate(zip(sources, targets, strict=True))
    ]
    for copy in copies:
        copy.start()
    return copies


def as_column(line):
    return jnp.concatenate(
        [
            jnp.broadcast_to(line[:, k : k + LANES], (LANES, LANES)).T
            for k in range(0, line.shape[1], LANES)
        ],
        0,
    )


def own_rows(place):
    return pl.ds(pl.multiple_of(LINES_AT + place * LINE_ROWS, LINE_ROWS), LINE_ROWS)


def join_kernel(limbs_ref, out_ref):
    rows = out_ref.shape[0]
    low = (limbs_ref[pl.ds(0, rows, stride=2), :] * 65536.0).astype(jnp.int32)
    high = (limbs_ref[pl.ds(1, rows, stride=2), :] * 65536.0).astype(jnp.int32)
    joined = (high << 16) + low
    out_ref[...] = jnp.where(joined > HALF, joined - MODULUS, joined)


def table_kernel(
    place_ref, shift_ref, powers_hbm, out_hbm, own_ref, shift_table_ref, ext_ref, sems
):
    place = place_ref[0]
    own = load([powers_hbm.at[own_rows(place)]], [own_ref], sems.at[pl.ds(0, 1)])

    first = jnp.full((8, LANES), shift_ref[0], jnp.int32)
    square = jnp.where(first > HALF, first - MODULUS, first)
    inverse_len = int(centered(np.int64(pow(TRACE_LEN, MODULUS - 2, MODULUS))))
    factor = jnp.full((8, LANES), inverse_len, jnp.int32)
    rows = lax.broadcasted_iota(jnp.int32, (SIDE, LANES), 0)
    column = jnp.ones((SIDE, LANES), jnp.int32)
    cols = lax.broadcasted_iota(jnp.int32, (8, SIDE), 1)
    line = None
    for bit in range(23):
        lifted = lift(square)
        if bit < 7:
            factor = jnp.where(place >> bit & 1 == 1, near_mul(factor, square, lifted), factor)
        elif bit < 15:
            plain_row, lifted_row = square[0:1], lifted[0:1]
            column = jnp.where(
                rows >> (bit - 7) & 1 == 1, near_mul(column, plain_row, lifted_row), column
            )
        else:
            if line is None:
                line = jnp.concatenate([factor] * (SIDE // LANES), 1)
            plain_row = jnp.concatenate([square] * (SIDE // LANES), 1)
            lifted_row = jnp.concatenate([lifted] * (SIDE // LANES), 1)
            line = jnp.where(
                cols >> (bit - 15) & 1 == 1, near_mul(line, plain_row, lifted_row), line
            )
        square = near_mul(square, square, lifted)
    line_lifted = lift(line)
    for k in range(SIDE // LANES):
        cols = slice(k * LANES, (k + 1) * LANES)
        value = near_mul(column, line[0:1, cols], line_lifted[0:1, cols])
        shift_table_ref[:, cols] = value
        shift_table_ref[:, SIDE + k * LANES : SIDE + (k + 1) * LANES] = lift(value)
    stores = load(
        [shift_table_ref], [out_hbm.at[pl.ds(2 * SIDE, SIDE)]], sems.at[pl.ds(1, 1)]
    )

    own[0].wait()
    column = as_column(own_ref[8:9, 0:SIDE])
    for k in range(LONG // LANES):
        cols = slice(k * LANES, (k + 1) * LANES)
        value = near_mul(column, own_ref[0:1, cols], own_ref[1:2, cols])
        ext_ref[0:SIDE, cols] = value
        ext_ref[SIDE:, cols] = lift(value)
    stores += load([ext_ref], [out_hbm.at[pl.ds(0, 2 * SIDE)]], sems.at[pl.ds(2, 1)])
    for copy in stores:
        copy.wait()


def gather_rows(ref, lines, per_line):
    return jnp.concatenate(
        [ref[pl.ds(k, lines, stride=per_line), :] for k in range(per_line)], 1
    )


def scatter_rows(ref, value, per_line, first=0):
    lines = value.shape[0]
    for k in range(value.shape[1] // LANES):
        ref[pl.ds(first + k, lines, stride=per_line), :] = value[:, k * LANES : (k + 1) * LANES]


def group_matrix(matrices_hbm, index):
    size = LIMBS * GROUP
    return matrices_hbm.at[pl.ds(2 * LIMBS * SIDE + index * size, size), pl.ds(0, size)]


def group_products(in_ref, matrix_ref, ready, finish):
    per_line = in_ref.shape[0] // GROUP
    step = 2
    splits = [
        digits(
            jnp.concatenate(
                [in_ref[pl.ds(first + k, GROUP, stride=per_line), :] for k in range(step)], 1
            ),
            0,
        )
        for first in range(0, per_line, step)
    ]
    ready()
    last = None
    for index, split in enumerate(splits):
        result = dot(matrix_ref[...], split)
        if last is not None:
            finish((index - 1) * step, from_rows(last, GROUP))
        last = result
    finish((len(splits) - 1) * step, from_rows(last, GROUP))


def group_back_kernel(
    place_ref,
    in_ref,
    matrices_hbm,
    powers_hbm,
    made_hbm,
    out_ref,
    matrix_ref,
    own_ref,
    base_ref,
    sems,
):
    copies = load(
        [
            group_matrix(matrices_hbm, 0),
            powers_hbm.at[own_rows(place_ref[0])],
            powers_hbm.at[pl.ds(768, 2 * GROUP)],
        ],
        [matrix_ref, own_ref, base_ref],
        sems,
    )
    columns = []

    def ready():
        for copy in copies:
            copy.wait()
        for row in (8, 9):
            column = as_column(own_ref[row : row + 1, SIDE : SIDE + LANES])
            columns.append(jnp.concatenate([column, column], 1))

    def finish(first, value):
        cols = slice(first * LANES, first * LANES + value.shape[1])
        value = paired_mul(value, base_ref[0:GROUP, cols], base_ref[GROUP:, cols])
        value = paired_mul(value, *columns)
        scatter_rows(out_ref, value, in_ref.shape[0] // GROUP, first)

    group_products(in_ref, matrix_ref, ready, finish)


def group_fwd_kernel(in_ref, matrices_hbm, out_ref, matrix_ref, sems):
    copies = load([group_matrix(matrices_hbm, 1)], [matrix_ref], sems)

    def finish(first, value):
        value = jnp.where(value < 0, value + MODULUS, value)
        value = jnp.where(value >= MODULUS, value - MODULUS, value)
        value = jnp.where(value < 0, value + MODULUS, value)
        scatter_rows(out_ref, value, in_ref.shape[0] // GROUP, first)

    group_products(in_ref, matrix_ref, copies[0].wait, finish)


def middle_kernel(
    in_ref,
    matrices_hbm,
    powers_hbm,
    made_hbm,
    out_ref,
    side_back_ref,
    mid_back_ref,
    shift_ref,
    long_fwd_t_ref,
    mid_fwd_ref,
    side_fwd_ref,
    ext_ref,
    sems,
):
    wide = LIMBS * SIDE
    part = wide // SPLIT_OUT
    rows = SIDE // SPLIT_OUT
    cols = LONG // SPLIT_OUT
    back = (((1,), (1,)), ((), ()))
    copies = load(
        [
            matrices_hbm.at[pl.ds(wide, wide), pl.ds(0, wide)],
            powers_hbm.at[pl.ds(2 * SIDE, SIDE)],
            made_hbm.at[pl.ds(2 * SIDE, SIDE)],
            matrices_hbm.at[pl.ds(0, wide)],
            powers_hbm.at[pl.ds(0, 2 * SIDE)],
            matrices_hbm.at[pl.ds(wide, wide), pl.ds(wide, wide)],
            made_hbm.at[pl.ds(0, 2 * SIDE)],
        ],
        [
            side_back_ref,
            mid_back_ref,
            shift_ref,
            long_fwd_t_ref,
            mid_fwd_ref,
            side_fwd_ref,
            ext_ref,
        ],
        sems,
    )

    def first(k, split):
        return dot(side_back_ref[k * part : (k + 1) * part, :], split)

    def after_first(k, result):
        here = slice(k * rows, (k + 1) * rows)
        result = from_rows(result, rows)
        return digits(
            paired_mul(result, mid_back_ref[here, 0:SIDE], mid_back_ref[here, SIDE:]), 1
        )

    def second(split):
        return lax.dot_general(
            split, side_back_ref[...], back, preferred_element_type=jnp.float32
        )

    def after_second(k, result):
        here = slice(k * rows, (k + 1) * rows)
        half = SIDE // SPLIT_OUT
        result = jnp.concatenate(
            [from_cols(result[:, n * part : (n + 1) * part], half) for n in range(SPLIT_OUT)], 1
        )
        return digits(paired_mul(result, shift_ref[here, 0:SIDE], shift_ref[here, SIDE:]), 1)

    split = digits(gather_rows(in_ref, SIDE, SIDE // LANES), 0)
    for copy in copies[:3]:
        copy.wait()
    one = first(0, split)
    two = first(1, split)
    one = second(after_first(0, one))
    two = second(after_first(1, two))
    one = after_second(0, one)
    two = after_second(1, two)
    split = jnp.concatenate([one, two], 0)
    for copy in copies[3:]:
        copy.wait()

    def third(k):
        return dot(split, long_fwd_t_ref[:, k * wide : (k + 1) * wide])

    def after_third(k, result):
        here = slice(k * cols, (k + 1) * cols)
        result = from_cols(result, cols)
        return digits(paired_mul(result, mid_fwd_ref[0:SIDE, here], mid_fwd_ref[SIDE:, here]), 0)

    def fourth(split):
        return dot(side_fwd_ref[...], split)

    def after_fourth(k, result):
        here = slice(k * cols, (k + 1) * cols)
        result = from_rows(result, SIDE)
        result = paired_mul(result, ext_ref[0:SIDE, here], ext_ref[SIDE:, here])
        scatter_rows(out_ref, result, LONG // LANES, k * cols // LANES)

    one = third(0)
    two = third(1)
    one = fourth(after_third(0, one))
    two = fourth(after_third(1, two))
    after_fourth(0, one)
    after_fourth(1, two)


def limbs_kernel(in_ref, out_ref):
    value = in_ref[...]
    rows = in_ref.shape[0]
    scale = np.float32(1.0 / 65536.0)
    out_ref[pl.ds(0, rows, stride=2), :] = (value & 65535).astype(jnp.float32) * scale
    out_ref[pl.ds(1, rows, stride=2), :] = (value >> 16).astype(jnp.float32) * scale


def exchange(rows):
    blocks = rows.reshape(GROUP, rows.shape[0] // GROUP, LANES)
    moved = lax.all_to_all(blocks, "rows", split_axis=0, concat_axis=0, tiled=True)
    return moved.reshape(rows.shape)


def on_device(trace_limbs, coset_shift):
    matrices, powers = (jnp.asarray(table) for table in tables())
    place = lax.axis_index("rows").astype(jnp.int32).reshape(1)
    rows = LOCAL // LANES
    wide = LIMBS * SIDE
    smem = pl.BlockSpec(memory_space=pltpu.SMEM)
    vmem = pl.BlockSpec(memory_space=pltpu.VMEM)
    anywhere = pl.BlockSpec(memory_space=pl.ANY)

    def ints(*shape):
        return jax.ShapeDtypeStruct(shape, jnp.int32)

    def limb(*shape):
        return jax.ShapeDtypeStruct(shape, jnp.bfloat16)

    def call(name, body, out_shape, in_specs, scratch=(), sems=0, cost=1, out_spec=vmem):
        scratch = [pltpu.VMEM(a.shape, a.dtype) for a in scratch]
        if sems:
            scratch.append(pltpu.SemaphoreType.DMA((sems,)))
        return pl.pallas_call(
            body,
            out_shape=out_shape,
            in_specs=in_specs,
            out_specs=out_spec,
            scratch_shapes=scratch,
            compiler_params=pltpu.CompilerParams(vmem_limit_bytes=48 << 20),
            cost_estimate=pl.CostEstimate(
                flops=cost * 1_000_000, bytes_accessed=1 << 20, transcendentals=0
            ),
            name=name,
        )

    limbs = trace_limbs.reshape(2, rows, LANES).transpose(1, 0, 2).reshape(2 * rows, LANES)
    values = call("join_limbs", join_kernel, ints(rows, LANES), [vmem])(limbs)
    made = call(
        "power_tables",
        table_kernel,
        ints(TABLE_ROWS, LONG),
        [smem, smem, anywhere],
        [ints(LINE_ROWS, LONG), ints(SIDE, LONG), ints(2 * SIDE, LONG)],
        3,
        300,
        anywhere,
    )(place, coset_shift, powers)
    columns = exchange(values)
    columns = call(
        "group_back",
        group_back_kernel,
        ints(rows, LANES),
        [smem, vmem, anywhere, anywhere, anywhere],
        [limb(LIMBS * GROUP, LIMBS * GROUP), ints(LINE_ROWS, LONG), ints(2 * GROUP, LONG)],
        3,
        300,
    )(place, columns, matrices, powers, made)
    block = exchange(columns)
    extended = call(
        "block_transforms",
        middle_kernel,
        ints(2 * rows, LANES),
        [vmem, anywhere, anywhere, anywhere],
        [
            limb(wide, wide),
            ints(SIDE, LONG),
            ints(SIDE, LONG),
            limb(wide, 2 * wide),
            ints(2 * SIDE, LONG),
            limb(wide, wide),
            ints(2 * SIDE, LONG),
        ],
        7,
        4000,
    )(block, matrices, powers, made)
    columns = exchange(extended)
    columns = call(
        "group_fwd",
        group_fwd_kernel,
        ints(2 * rows, LANES),
        [vmem, anywhere],
        [limb(LIMBS * GROUP, LIMBS * GROUP)],
        1,
        500,
    )(columns, matrices)
    ordered = exchange(columns)
    pairs = call(
        "split_limbs", limbs_kernel, jax.ShapeDtypeStruct((4 * rows, LANES), jnp.float32), [vmem]
    )(ordered)
    return pairs.reshape(2 * rows, 2, LANES).transpose(1, 0, 2).reshape(2, 2 * rows * LANES)


def solution(mesh):
    placed = (P(None, ("cols", "rows")), P())
    return jax.shard_map(
        on_device, mesh=mesh, in_specs=placed, out_specs=P(None, ("cols", "rows")), check_vma=False
    )
```

```python
import functools

import jax
import jax.numpy as jnp
import ml_dtypes
import numpy as np
from jax import lax
from jax.experimental import pallas as pl
from jax.experimental.pallas import tpu as pltpu
from jax.sharding import PartitionSpec as P

LEN_A = 2048
LEN_B = 4096
MODULUS = 2013265921
HALF = MODULUS // 2
SPLIT = 15
LIMBS = 4
BYTE_BIAS = -2139062144

TRACE_LEN = LEN_A * LEN_B
EXT_LEN = 2 * TRACE_LEN
GROUP = 128
SIDE = 256
LONG = 2 * SIDE
LOCAL = SIDE * SIDE
LANES = 128


def unity_root(length):
    return pow(pow(31, 15, MODULUS), (1 << 27) // length, MODULUS)


BACK_ROOT = pow(unity_root(TRACE_LEN), MODULUS - 2, MODULUS)
FWD_ROOT = unity_root(EXT_LEN)


def powers_of(base, exponents):
    exponents = np.asarray(exponents, dtype=np.int64)
    result = np.ones(exponents.shape, dtype=np.int64)
    square = base % MODULUS
    for bit in range(int(exponents.max(initial=0)).bit_length()):
        result = np.where(exponents >> bit & 1 == 1, mul_mod(result, square), result)
        square = square * square % MODULUS
    return result


def mul_mod(left, right):
    return left * right % MODULUS


def centered(values):
    values = values % MODULUS
    return np.where(values > HALF, values - MODULUS, values)


def both_halves(values):
    return np.stack([centered(values), centered(mul_mod(values, 1 << SPLIT))]).astype(np.int32)


def limbs_of(values):
    rest = centered(values)
    digits = []
    for _ in range(LIMBS):
        digit = (rest + 128) % 256 - 128
        digits.append(digit)
        rest = (rest - digit) // 256
    return np.stack(digits)


def limb_matrix(matrix):
    blocks = np.stack([limbs_of(mul_mod(matrix, 256**a)) for a in range(LIMBS)], axis=2)
    out_len, in_len = matrix.shape
    return np.ascontiguousarray(
        blocks.reshape(LIMBS * out_len, LIMBS * in_len).astype(ml_dtypes.bfloat16)
    )


def dft_matrix(root, out_len, in_len):
    return powers_of(root, np.arange(out_len)[:, None] * np.arange(in_len)[None, :])


SPLIT_OUT = 2
MATRIX_ROWS = 4 * LIMBS * SIDE + LIMBS * GROUP
TABLE_ROWS = 4096
LINE_ROWS = 16
LINES_AT = 1024


def in_parts(matrix, count):
    rows, cols = matrix.shape
    parts = matrix.reshape(LIMBS, SPLIT_OUT, count // SPLIT_OUT, cols).transpose(1, 0, 2, 3)
    return parts.reshape(rows, cols)


@functools.cache
def tables():
    lines = np.arange(GROUP)
    side = np.arange(SIDE)
    long = np.arange(LONG)
    tile = np.arange(LOCAL // GROUP)
    back_side = pow(unity_root(SIDE), MODULUS - 2, MODULUS)
    root_group = unity_root(GROUP)
    back_group = pow(root_group, MODULUS - 2, MODULUS)
    back_local = pow(unity_root(LOCAL), MODULUS - 2, MODULUS)
    side_back = limb_matrix(dft_matrix(back_side, SIDE, SIDE))
    wide = LIMBS * SIDE
    matrices = np.zeros((MATRIX_ROWS, wide), ml_dtypes.bfloat16)
    long_fwd = in_parts(limb_matrix(dft_matrix(unity_root(LONG), LONG, SIDE)), LONG)
    matrices[:wide] = long_fwd[:wide].T
    matrices[wide : 2 * wide] = long_fwd[wide:].T
    matrices[2 * wide : 3 * wide] = in_parts(side_back, SIDE)
    matrices[3 * wide : 4 * wide] = side_back.T
    matrices[4 * wide :] = np.concatenate(
        [limb_matrix(dft_matrix(root, GROUP, GROUP)) for root in (back_group, root_group)], axis=1
    )

    powers = np.zeros((TABLE_ROWS, LONG), np.int32)
    powers[0:512] = both_halves(
        powers_of(unity_root(2 * LOCAL), side[:, None] * long[None, :])
    ).reshape(512, LONG)
    powers[512:768] = np.concatenate(
        both_halves(powers_of(back_local, side[:, None] * side[None, :])), axis=1
    )
    powers[768:1024] = both_halves(
        powers_of(BACK_ROOT, lines[:, None] * tile[None, :])
    ).reshape(256, LONG)
    own = np.zeros((GROUP, LINE_ROWS, LONG), np.int32)

    def place_pair(root, exponents, row, lane):
        pair = both_halves(powers_of(root, lines[:, None] * exponents[None, :]))
        own[:, row : row + 2, lane : lane + exponents.size] = pair.transpose(1, 0, 2)

    place_pair(FWD_ROOT, long, 0, 0)
    place_pair(FWD_ROOT, LONG * (-side % SIDE), 8, 0)
    place_pair(BACK_ROOT, tile.size * lines, 8, SIDE)
    powers[LINES_AT : LINES_AT + GROUP * LINE_ROWS] = own.reshape(GROUP * LINE_ROWS, LONG)
    return matrices, powers


def toward_zero(value):
    return value.astype(jnp.int32)


def to_nearest(value):
    return jnp.floor(value + 0.5).astype(jnp.int32)


def paired_mul(value, plain, lifted, whole=toward_zero):
    high = value >> SPLIT
    low = value & ((1 << SPLIT) - 1)
    scale = np.float32(1.0 / MODULUS)
    upper = high.astype(jnp.float32) * lifted.astype(jnp.float32)
    lower = low.astype(jnp.float32) * plain.astype(jnp.float32)
    return high * lifted + low * plain - whole((upper + lower) * scale) * MODULUS


near_mul = functools.partial(paired_mul, whole=to_nearest)


def lift(value):
    once, twice = (int(centered(np.int64(1 << k * SPLIT))) for k in (1, 2))
    return near_mul(value, jnp.int32(once), jnp.int32(twice))


def digits(value, axis):
    biased = (value + jnp.int32(BYTE_BIAS)) ^ jnp.int32(BYTE_BIAS)
    parts = [(biased << (24 - 8 * k)) >> 24 for k in range(LIMBS - 1)] + [biased >> 24]
    return jnp.concatenate([part.astype(jnp.float32).astype(jnp.bfloat16) for part in parts], axis)


def combine(part0, part1, part2, part3):
    estimate = (
        part3 * np.float32(2.0**24 / MODULUS)
        + part2 * np.float32(2.0**16 / MODULUS)
        + part1 * np.float32(2.0**8 / MODULUS)
    )
    whole = [part.astype(jnp.int32) for part in (part0, part1, part2, part3)]
    total = whole[0] + (whole[1] << 8) + (whole[2] << 16) + (whole[3] << 24)
    return total - toward_zero(estimate) * MODULUS


def dot(left, right):
    return jnp.dot(left, right, preferred_element_type=jnp.float32)


def from_rows(result, count):
    return combine(*(result[k * count : (k + 1) * count] for k in range(LIMBS)))


def from_cols(result, count):
    return combine(*(result[:, k * count : (k + 1) * count] for k in range(LIMBS)))


def load(sources, targets, sems):
    copies = [
        pltpu.make_async_copy(source, target, sems.at[k])
        for k, (source, target) in enumerate(zip(sources, targets, strict=True))
    ]
    for copy in copies:
        copy.start()
    return copies


def as_column(line):
    return jnp.concatenate(
        [
            jnp.broadcast_to(line[:, k : k + LANES], (LANES, LANES)).T
            for k in range(0, line.shape[1], LANES)
        ],
        0,
    )


def own_rows(place):
    return pl.ds(pl.multiple_of(LINES_AT + place * LINE_ROWS, LINE_ROWS), LINE_ROWS)


def join_kernel(limbs_hbm, out_hbm, limbs_ref, out_ref, in_sems, out_sems):
    parts = in_sems.shape[0]
    rows = out_ref.shape[0] // parts
    pairs = [pl.ds(2 * rows * k, 2 * rows) for k in range(parts)]
    lines = [pl.ds(rows * k, rows) for k in range(parts)]
    copies = load([limbs_hbm.at[r] for r in pairs], [limbs_ref.at[r] for r in pairs], in_sems)
    stores = []
    for k, copy in enumerate(copies):
        copy.wait()
        low = limbs_ref[pl.ds(2 * rows * k, rows, stride=2), :] * 65536.0
        high = limbs_ref[pl.ds(2 * rows * k + 1, rows, stride=2), :] * 65536.0
        joined = (high.astype(jnp.int32) << 16) + low.astype(jnp.int32)
        out_ref[lines[k], :] = jnp.where(joined > HALF, joined - MODULUS, joined)
        stores += load([out_ref.at[lines[k]]], [out_hbm.at[lines[k]]], out_sems.at[pl.ds(k, 1)])
    for copy in stores:
        copy.wait()


def table_kernel(
    place_ref, shift_ref, powers_hbm, out_hbm, own_ref, shift_table_ref, ext_ref, sems
):
    place = place_ref[0]
    own = load([powers_hbm.at[own_rows(place)]], [own_ref], sems.at[pl.ds(0, 1)])

    first = jnp.full((8, LANES), shift_ref[0], jnp.int32)
    square = jnp.where(first > HALF, first - MODULUS, first)
    inverse_len = int(centered(np.int64(pow(TRACE_LEN, MODULUS - 2, MODULUS))))
    factor = jnp.full((8, LANES), inverse_len, jnp.int32)
    rows = lax.broadcasted_iota(jnp.int32, (SIDE, LANES), 0)
    column = jnp.ones((SIDE, LANES), jnp.int32)
    cols = lax.broadcasted_iota(jnp.int32, (8, SIDE), 1)
    line = None
    for bit in range(23):
        lifted = lift(square)
        if bit < 7:
            factor = jnp.where(place >> bit & 1 == 1, near_mul(factor, square, lifted), factor)
        elif bit < 15:
            plain_row, lifted_row = square[0:1], lifted[0:1]
            column = jnp.where(
                rows >> (bit - 7) & 1 == 1, near_mul(column, plain_row, lifted_row), column
            )
        else:
            if line is None:
                line = jnp.concatenate([factor] * (SIDE // LANES), 1)
            plain_row = jnp.concatenate([square] * (SIDE // LANES), 1)
            lifted_row = jnp.concatenate([lifted] * (SIDE // LANES), 1)
            line = jnp.where(
                cols >> (bit - 15) & 1 == 1, near_mul(line, plain_row, lifted_row), line
            )
        square = near_mul(square, square, lifted)
    line_lifted = lift(line)
    for k in range(SIDE // LANES):
        cols = slice(k * LANES, (k + 1) * LANES)
        value = near_mul(column, line[0:1, cols], line_lifted[0:1, cols])
        shift_table_ref[:, cols] = value
        shift_table_ref[:, SIDE + k * LANES : SIDE + (k + 1) * LANES] = lift(value)
    stores = load(
        [shift_table_ref], [out_hbm.at[pl.ds(2 * SIDE, SIDE)]], sems.at[pl.ds(1, 1)]
    )

    own[0].wait()
    column = as_column(own_ref[8:9, 0:SIDE])
    for k in range(LONG // LANES):
        cols = slice(k * LANES, (k + 1) * LANES)
        value = near_mul(column, own_ref[0:1, cols], own_ref[1:2, cols])
        ext_ref[0:SIDE, cols] = value
        ext_ref[SIDE:, cols] = lift(value)
    stores += load([ext_ref], [out_hbm.at[pl.ds(0, 2 * SIDE)]], sems.at[pl.ds(2, 1)])
    for copy in stores:
        copy.wait()


def gather_rows(ref, lines, per_line):
    return jnp.concatenate(
        [ref[pl.ds(k, lines, stride=per_line), :] for k in range(per_line)], 1
    )


def scatter_rows(ref, value, per_line, first=0):
    lines = value.shape[0]
    for k in range(value.shape[1] // LANES):
        ref[pl.ds(first + k, lines, stride=per_line), :] = value[:, k * LANES : (k + 1) * LANES]


def group_matrix(matrices_hbm, index):
    size = LIMBS * GROUP
    return matrices_hbm.at[pl.ds(4 * LIMBS * SIDE, size), pl.ds(index * size, size)]


def group_products(in_ref, matrix_ref, ready, finish):
    per_line = in_ref.shape[0] // GROUP
    step = 2
    splits = [
        digits(
            jnp.concatenate(
                [in_ref[pl.ds(first + k, GROUP, stride=per_line), :] for k in range(step)], 1
            ),
            0,
        )
        for first in range(0, per_line, step)
    ]
    ready()
    last = None
    for index, split in enumerate(splits):
        result = dot(matrix_ref[...], split)
        if last is not None:
            finish((index - 1) * step, from_rows(last, GROUP))
        last = result
    finish((len(splits) - 1) * step, from_rows(last, GROUP))


def group_back_kernel(
    place_ref,
    in_ref,
    matrices_hbm,
    powers_hbm,
    made_hbm,
    out_ref,
    side_back_ref,
    mid_back_ref,
    shift_ref,
    matrix_ref,
    own_ref,
    base_ref,
    sems,
    next_sems,
):
    copies = load(
        [
            group_matrix(matrices_hbm, 0),
            powers_hbm.at[own_rows(place_ref[0])],
            powers_hbm.at[pl.ds(768, 2 * GROUP)],
        ],
        [matrix_ref, own_ref, base_ref],
        sems,
    )
    brought = load(
        [
            matrices_hbm.at[pl.ds(2 * LIMBS * SIDE, LIMBS * SIDE)],
            powers_hbm.at[pl.ds(2 * SIDE, SIDE)],
            made_hbm.at[pl.ds(2 * SIDE, SIDE)],
        ],
        [side_back_ref, mid_back_ref, shift_ref],
        next_sems,
    )
    columns = []

    def ready():
        for copy in copies:
            copy.wait()
        for row in (8, 9):
            column = as_column(own_ref[row : row + 1, SIDE : SIDE + LANES])
            columns.append(jnp.concatenate([column, column], 1))

    def finish(first, value):
        cols = slice(first * LANES, first * LANES + value.shape[1])
        value = paired_mul(value, base_ref[0:GROUP, cols], base_ref[GROUP:, cols])
        value = paired_mul(value, *columns)
        scatter_rows(out_ref, value, in_ref.shape[0] // GROUP, first)

    group_products(in_ref, matrix_ref, ready, finish)
    for copy in brought:
        copy.wait()


def group_fwd_kernel(in_ref, matrix_ref, out_ref):
    def finish(first, value):
        value = jnp.where(value < 0, value + MODULUS, value)
        value = jnp.where(value >= MODULUS, value - MODULUS, value)
        value = jnp.where(value < 0, value + MODULUS, value)
        scatter_rows(out_ref, value, in_ref.shape[0] // GROUP, first)

    group_products(in_ref, matrix_ref, lambda: None, finish)


def middle_kernel(
    in_ref,
    side_back_ref,
    mid_back_ref,
    shift_ref,
    matrices_hbm,
    powers_hbm,
    made_hbm,
    out_ref,
    group_fwd_ref,
    side_back_t_ref,
    long_fwd_t_ref,
    mid_fwd_ref,
    ext_ref,
    sems,
):
    wide = LIMBS * SIDE
    part = wide // SPLIT_OUT
    rows = SIDE // SPLIT_OUT
    cols = LONG // SPLIT_OUT
    copies = load(
        [
            matrices_hbm.at[pl.ds(3 * wide, wide)],
            matrices_hbm.at[pl.ds(0, wide)],
            matrices_hbm.at[pl.ds(wide, wide)],
            powers_hbm.at[pl.ds(0, 2 * SIDE)],
            made_hbm.at[pl.ds(0, 2 * SIDE)],
            group_matrix(matrices_hbm, 1),
        ],
        [
            side_back_t_ref,
            long_fwd_t_ref.at[pl.ds(0, wide)],
            long_fwd_t_ref.at[pl.ds(wide, wide)],
            mid_fwd_ref,
            ext_ref,
            group_fwd_ref,
        ],
        sems,
    )

    def first(k, split):
        return dot(side_back_ref[k * part : (k + 1) * part, :], split)

    def after_first(k, result):
        here = slice(k * rows, (k + 1) * rows)
        result = from_rows(result, rows)
        return digits(
            paired_mul(result, mid_back_ref[here, 0:SIDE], mid_back_ref[here, SIDE:]), 1
        )

    def second(split):
        return dot(split, side_back_t_ref[...])

    def after_second(k, result):
        here = slice(k * rows, (k + 1) * rows)
        result = from_cols(result, SIDE)
        return digits(paired_mul(result, shift_ref[here, 0:SIDE], shift_ref[here, SIDE:]), 1)

    split = digits(gather_rows(in_ref, SIDE, SIDE // LANES), 0)
    one = first(0, split)
    two = first(1, split)
    one = after_first(0, one)
    copies[0].wait()
    one = second(one)
    two = after_first(1, two)
    one = after_second(0, one)
    two = second(two)
    two = after_second(1, two)
    split = jnp.concatenate([one, two], 0)
    copies[1].wait()
    copies[2].wait()

    def third(k):
        return dot(split, long_fwd_t_ref[k * wide : (k + 1) * wide, :])

    def after_third(k, result):
        here = slice(k * cols, (k + 1) * cols)
        result = from_cols(result, cols)
        return digits(paired_mul(result, mid_fwd_ref[0:SIDE, here], mid_fwd_ref[SIDE:, here]), 0)

    def fourth(split):
        return dot(side_back_ref[...], split)

    def after_fourth(k, result):
        here = slice(k * cols, (k + 1) * cols)
        result = jnp.concatenate(
            [from_rows(result[n * part : (n + 1) * part], rows) for n in range(SPLIT_OUT)], 0
        )
        result = paired_mul(result, ext_ref[0:SIDE, here], ext_ref[SIDE:, here])
        scatter_rows(out_ref, result, LONG // LANES, k * cols // LANES)

    one = third(0)
    for copy in copies[3:]:
        copy.wait()
    two = third(1)
    one = fourth(after_third(0, one))
    two = after_third(1, two)
    after_fourth(0, one)
    two = fourth(two)
    after_fourth(1, two)


def limbs_kernel(in_ref, out_hbm, out_ref, sems):
    scale = np.float32(1.0 / 65536.0)
    per_line = LONG // LANES
    parts = sems.shape[0]
    rows = out_ref.shape[0] // parts
    stores = []
    for line in range(SIDE):
        value = in_ref[pl.ds(-line % SIDE * per_line, per_line), :]
        first = 2 * per_line * line
        low = (value & 65535).astype(jnp.float32) * scale
        high = (value >> 16).astype(jnp.float32) * scale
        out_ref[pl.ds(first, per_line, stride=2), :] = low
        out_ref[pl.ds(first + 1, per_line, stride=2), :] = high
        done = first + 2 * per_line
        if done % rows == 0:
            part = pl.ds(done - rows, rows)
            stores += load(
                [out_ref.at[part]], [out_hbm.at[part]], sems.at[pl.ds(len(stores), 1)]
            )
    for copy in stores:
        copy.wait()


def exchange(rows):
    blocks = rows.reshape(GROUP, rows.shape[0] // GROUP, LANES)
    moved = lax.all_to_all(blocks, "rows", split_axis=0, concat_axis=0, tiled=True)
    return moved.reshape(rows.shape)


def on_device(trace_limbs, coset_shift):
    matrices, powers = (jnp.asarray(table) for table in tables())
    place = lax.axis_index("rows").astype(jnp.int32).reshape(1)
    rows = LOCAL // LANES
    wide = LIMBS * SIDE
    smem = pl.BlockSpec(memory_space=pltpu.SMEM)
    vmem = pl.BlockSpec(memory_space=pltpu.VMEM)
    anywhere = pl.BlockSpec(memory_space=pl.ANY)

    def ints(*shape):
        return jax.ShapeDtypeStruct(shape, jnp.int32)

    def limb(*shape):
        return jax.ShapeDtypeStruct(shape, jnp.bfloat16)

    def call(
        name, body, out_shape, in_specs, scratch=(), sems=(), cost=1, out_specs=vmem, megabytes=48
    ):
        scratch = [pltpu.VMEM(a.shape, a.dtype) for a in scratch]
        scratch += [pltpu.SemaphoreType.DMA((count,)) for count in sems]
        return pl.pallas_call(
            body,
            out_shape=out_shape,
            in_specs=in_specs,
            out_specs=out_specs,
            scratch_shapes=scratch,
            compiler_params=pltpu.CompilerParams(vmem_limit_bytes=megabytes << 20),
            cost_estimate=pl.CostEstimate(
                flops=cost * 1_000_000, bytes_accessed=1 << 20, transcendentals=0
            ),
            name=name,
        )

    limbs = trace_limbs.reshape(2, rows, LANES).transpose(1, 0, 2).reshape(2 * rows, LANES)
    values = call(
        "join_limbs",
        join_kernel,
        ints(rows, LANES),
        [anywhere],
        [limbs, ints(rows, LANES)],
        (4, 4),
        out_specs=anywhere,
        megabytes=60,
    )(limbs)
    made = call(
        "power_tables",
        table_kernel,
        ints(TABLE_ROWS, LONG),
        [smem, smem, anywhere],
        [ints(LINE_ROWS, LONG), ints(SIDE, LONG), ints(2 * SIDE, LONG)],
        (3,),
        300,
        anywhere,
    )(place, coset_shift, powers)
    columns = exchange(values)
    columns, *brought = call(
        "group_back",
        group_back_kernel,
        [ints(rows, LANES), limb(wide, wide), ints(SIDE, LONG), ints(SIDE, LONG)],
        [smem, vmem, anywhere, anywhere, anywhere],
        [limb(LIMBS * GROUP, LIMBS * GROUP), ints(LINE_ROWS, LONG), ints(2 * GROUP, LONG)],
        (3, 3),
        300,
        [vmem] * 4,
    )(place, columns, matrices, powers, made)
    block = exchange(columns)
    extended, group_fwd = call(
        "block_transforms",
        middle_kernel,
        [ints(2 * rows, LANES), limb(LIMBS * GROUP, LIMBS * GROUP)],
        [vmem] * 4 + [anywhere] * 3,
        [
            limb(wide, wide),
            limb(2 * wide, wide),
            ints(2 * SIDE, LONG),
            ints(2 * SIDE, LONG),
        ],
        (6,),
        4000,
        [vmem] * 2,
    )(block, *brought, matrices, powers, made)
    columns = exchange(extended)
    columns = call("group_fwd", group_fwd_kernel, ints(2 * rows, LANES), [vmem] * 2, cost=500)(
        columns, group_fwd
    )
    ordered = exchange(columns)
    pairs = jax.ShapeDtypeStruct((4 * rows, LANES), jnp.float32)
    pairs = call(
        "split_limbs", limbs_kernel, pairs, [vmem], [pairs], (4,), out_specs=anywhere
    )(ordered)
    return pairs.reshape(2 * rows, 2, LANES).transpose(1, 0, 2).reshape(2, 2 * rows * LANES)


def solution(mesh):
    placed = (P(None, ("cols", "rows")), P())
    return jax.shard_map(
        on_device, mesh=mesh, in_specs=placed, out_specs=P(None, ("cols", "rows")), check_vma=False
    )
```

```python
import functools

import jax
import jax.numpy as jnp
import ml_dtypes
import numpy as np
from jax import lax
from jax.experimental import pallas as pl
from jax.experimental.pallas import tpu as pltpu
from jax.sharding import PartitionSpec as P

LEN_A = 2048
LEN_B = 4096
MODULUS = 2013265921
HALF = MODULUS // 2
SPLIT = 15
LIMBS = 4
BYTE_BIAS = -2139062144

TRACE_LEN = LEN_A * LEN_B
EXT_LEN = 2 * TRACE_LEN
GROUP = 128
SIDE = 256
LONG = 2 * SIDE
LOCAL = SIDE * SIDE
LANES = 128


def unity_root(length):
    return pow(pow(31, 15, MODULUS), (1 << 27) // length, MODULUS)


BACK_ROOT = pow(unity_root(TRACE_LEN), MODULUS - 2, MODULUS)
FWD_ROOT = unity_root(EXT_LEN)


def powers_of(base, exponents):
    exponents = np.asarray(exponents, dtype=np.int64)
    result = np.ones(exponents.shape, dtype=np.int64)
    square = base % MODULUS
    for bit in range(int(exponents.max(initial=0)).bit_length()):
        result = np.where(exponents >> bit & 1 == 1, mul_mod(result, square), result)
        square = square * square % MODULUS
    return result


def mul_mod(left, right):
    return left * right % MODULUS


def centered(values):
    values = values % MODULUS
    return np.where(values > HALF, values - MODULUS, values)


def both_halves(values):
    return np.stack([centered(values), centered(mul_mod(values, 1 << SPLIT))]).astype(np.int32)


def limbs_of(values):
    rest = centered(values)
    digits = []
    for _ in range(LIMBS):
        digit = (rest + 128) % 256 - 128
        digits.append(digit)
        rest = (rest - digit) // 256
    return np.stack(digits)


def limb_matrix(matrix):
    blocks = np.stack([limbs_of(mul_mod(matrix, 256**a)) for a in range(LIMBS)], axis=2)
    out_len, in_len = matrix.shape
    return np.ascontiguousarray(
        blocks.reshape(LIMBS * out_len, LIMBS * in_len).astype(ml_dtypes.bfloat16)
    )


def dft_matrix(root, out_len, in_len):
    return powers_of(root, np.arange(out_len)[:, None] * np.arange(in_len)[None, :])


SPLIT_OUT = 2
MATRIX_ROWS = 3 * LIMBS * SIDE + LIMBS * GROUP
TABLE_ROWS = 4096
LINE_ROWS = 16
LINES_AT = 1024


def in_parts(matrix, count):
    rows, cols = matrix.shape
    parts = matrix.reshape(LIMBS, SPLIT_OUT, count // SPLIT_OUT, cols).transpose(1, 0, 2, 3)
    return parts.reshape(rows, cols)


@functools.cache
def tables():
    lines = np.arange(GROUP)
    side = np.arange(SIDE)
    long = np.arange(LONG)
    tile = np.arange(LOCAL // GROUP)
    back_side = pow(unity_root(SIDE), MODULUS - 2, MODULUS)
    root_group = unity_root(GROUP)
    back_group = pow(root_group, MODULUS - 2, MODULUS)
    back_local = pow(unity_root(LOCAL), MODULUS - 2, MODULUS)
    side_back = limb_matrix(dft_matrix(back_side, SIDE, SIDE))
    wide = LIMBS * SIDE
    matrices = np.zeros((MATRIX_ROWS, wide), ml_dtypes.bfloat16)
    long_fwd = in_parts(limb_matrix(dft_matrix(unity_root(LONG), LONG, SIDE)), LONG)
    matrices[:wide] = long_fwd[:wide].T
    matrices[wide : 2 * wide] = long_fwd[wide:].T
    matrices[2 * wide : 3 * wide] = in_parts(side_back, SIDE)
    matrices[3 * wide :] = np.concatenate(
        [limb_matrix(dft_matrix(root, GROUP, GROUP)) for root in (back_group, root_group)], axis=1
    )

    powers = np.zeros((TABLE_ROWS, LONG), np.int32)
    powers[0:512] = both_halves(
        powers_of(unity_root(2 * LOCAL), side[:, None] * long[None, :])
    ).reshape(512, LONG)
    powers[512:768] = np.concatenate(
        both_halves(powers_of(back_local, side[:, None] * side[None, :])), axis=1
    )
    powers[768:1024] = both_halves(
        powers_of(BACK_ROOT, lines[:, None] * tile[None, :])
    ).reshape(256, LONG)
    own = np.zeros((GROUP, LINE_ROWS, LONG), np.int32)

    def place_pair(root, exponents, row, lane):
        pair = both_halves(powers_of(root, lines[:, None] * exponents[None, :]))
        own[:, row : row + 2, lane : lane + exponents.size] = pair.transpose(1, 0, 2)

    place_pair(FWD_ROOT, long, 0, 0)
    place_pair(FWD_ROOT, LONG * (-side % SIDE), 8, 0)
    place_pair(BACK_ROOT, tile.size * lines, 8, SIDE)
    powers[LINES_AT : LINES_AT + GROUP * LINE_ROWS] = own.reshape(GROUP * LINE_ROWS, LONG)
    return matrices, powers


def toward_zero(value):
    return value.astype(jnp.int32)


def to_nearest(value):
    return jnp.floor(value + 0.5).astype(jnp.int32)


def paired_mul(value, plain, lifted, whole=toward_zero):
    high = value >> SPLIT
    low = value & ((1 << SPLIT) - 1)
    scale = np.float32(1.0 / MODULUS)
    upper = high.astype(jnp.float32) * lifted.astype(jnp.float32)
    lower = low.astype(jnp.float32) * plain.astype(jnp.float32)
    return high * lifted + low * plain - whole((upper + lower) * scale) * MODULUS


near_mul = functools.partial(paired_mul, whole=to_nearest)


def lift(value):
    once, twice = (int(centered(np.int64(1 << k * SPLIT))) for k in (1, 2))
    return near_mul(value, jnp.int32(once), jnp.int32(twice))


def digits(value, axis):
    biased = (value + jnp.int32(BYTE_BIAS)) ^ jnp.int32(BYTE_BIAS)
    parts = [(biased << (24 - 8 * k)) >> 24 for k in range(LIMBS - 1)] + [biased >> 24]
    return jnp.concatenate([part.astype(jnp.float32).astype(jnp.bfloat16) for part in parts], axis)


def combine(part0, part1, part2, part3):
    estimate = (
        part3 * np.float32(2.0**24 / MODULUS)
        + part2 * np.float32(2.0**16 / MODULUS)
        + part1 * np.float32(2.0**8 / MODULUS)
    )
    whole = [part.astype(jnp.int32) for part in (part0, part1, part2, part3)]
    total = whole[0] + (whole[1] << 8) + (whole[2] << 16) + (whole[3] << 24)
    return total - toward_zero(estimate) * MODULUS


def dot(left, right):
    return jnp.dot(left, right, preferred_element_type=jnp.float32)


def from_rows(result, count):
    return combine(*(result[k * count : (k + 1) * count] for k in range(LIMBS)))


def from_cols(result, count):
    return combine(*(result[:, k * count : (k + 1) * count] for k in range(LIMBS)))


def load(sources, targets, sems):
    copies = [
        pltpu.make_async_copy(source, target, sems.at[k])
        for k, (source, target) in enumerate(zip(sources, targets, strict=True))
    ]
    for copy in copies:
        copy.start()
    return copies


def as_column(line):
    return jnp.concatenate(
        [
            jnp.broadcast_to(line[:, k : k + LANES], (LANES, LANES)).T
            for k in range(0, line.shape[1], LANES)
        ],
        0,
    )


def own_rows(place):
    return pl.ds(pl.multiple_of(LINES_AT + place * LINE_ROWS, LINE_ROWS), LINE_ROWS)


def tables_kernel(
    place_ref,
    shift_ref,
    matrices_hbm,
    powers_hbm,
    group_back_ref,
    base_ref,
    own_ref,
    side_back_ref,
    mid_back_ref,
    shift_cols_ref,
    shift_rows_ref,
    sems,
):
    place = place_ref[0]
    copies = load(
        [
            group_matrix(matrices_hbm, 0),
            powers_hbm.at[pl.ds(768, 2 * GROUP)],
            powers_hbm.at[own_rows(place)],
            matrices_hbm.at[pl.ds(2 * LIMBS * SIDE, LIMBS * SIDE)],
            powers_hbm.at[pl.ds(2 * SIDE, SIDE)],
        ],
        [group_back_ref, base_ref, own_ref, side_back_ref, mid_back_ref],
        sems,
    )

    first = jnp.full((8, LANES), shift_ref[0], jnp.int32)
    square = jnp.where(first > HALF, first - MODULUS, first)
    inverse_len = int(centered(np.int64(pow(TRACE_LEN, MODULUS - 2, MODULUS))))
    factor = jnp.full((8, LANES), inverse_len, jnp.int32)
    lines = lax.broadcasted_iota(jnp.int32, (SIDE, LANES), 0)
    column = jnp.ones((SIDE, LANES), jnp.int32)
    cols = lax.broadcasted_iota(jnp.int32, (8, SIDE), 1)
    line = None
    for bit in range(23):
        lifted = lift(square)
        if bit < 7:
            factor = jnp.where(place >> bit & 1 == 1, near_mul(factor, square, lifted), factor)
        elif bit < 15:
            plain_row, lifted_row = square[0:1], lifted[0:1]
            column = jnp.where(
                lines >> (bit - 7) & 1 == 1, near_mul(column, plain_row, lifted_row), column
            )
        else:
            if line is None:
                line = jnp.concatenate([factor] * (SIDE // LANES), 1)
            plain_row = jnp.concatenate([square] * (SIDE // LANES), 1)
            lifted_row = jnp.concatenate([lifted] * (SIDE // LANES), 1)
            line = jnp.where(
                cols >> (bit - 15) & 1 == 1, near_mul(line, plain_row, lifted_row), line
            )
        square = near_mul(square, square, lifted)
    shift_cols_ref[0:SIDE, :] = column
    shift_cols_ref[SIDE:, :] = lift(column)
    shift_rows_ref[0:8, :] = line
    shift_rows_ref[8:16, :] = lift(line)

    for copy in copies:
        copy.wait()


def join_kernel(limbs_ref, after_ref, out_ref):
    rows = out_ref.shape[0]
    low = (limbs_ref[pl.ds(0, rows, stride=2), :] * 65536.0).astype(jnp.int32)
    high = (limbs_ref[pl.ds(1, rows, stride=2), :] * 65536.0).astype(jnp.int32)
    joined = (high << 16) + low
    out_ref[...] = jnp.where(joined > HALF, joined - MODULUS, joined)


def gather_rows(ref, lines, per_line):
    return jnp.concatenate(
        [ref[pl.ds(k, lines, stride=per_line), :] for k in range(per_line)], 1
    )


def scatter_rows(ref, value, per_line, first=0):
    lines = value.shape[0]
    for k in range(value.shape[1] // LANES):
        ref[pl.ds(first + k, lines, stride=per_line), :] = value[:, k * LANES : (k + 1) * LANES]


def group_matrix(matrices_hbm, index):
    size = LIMBS * GROUP
    return matrices_hbm.at[pl.ds(3 * LIMBS * SIDE, size), pl.ds(index * size, size)]


def group_products(in_ref, matrix_ref, finish):
    per_line = in_ref.shape[0] // GROUP
    step = 2
    splits = [
        digits(
            jnp.concatenate(
                [in_ref[pl.ds(first + k, GROUP, stride=per_line), :] for k in range(step)], 1
            ),
            0,
        )
        for first in range(0, per_line, step)
    ]
    last = None
    for index, split in enumerate(splits):
        result = dot(matrix_ref[...], split)
        if last is not None:
            finish((index - 1) * step, from_rows(last, GROUP))
        last = result
    finish((len(splits) - 1) * step, from_rows(last, GROUP))


def group_back_kernel(in_ref, matrix_ref, base_ref, own_ref, out_ref):
    columns = [
        jnp.concatenate([as_column(own_ref[row : row + 1, SIDE : SIDE + LANES])] * 2, 1)
        for row in (8, 9)
    ]

    def finish(first, value):
        cols = slice(first * LANES, first * LANES + value.shape[1])
        value = paired_mul(value, base_ref[0:GROUP, cols], base_ref[GROUP:, cols])
        value = paired_mul(value, *columns)
        scatter_rows(out_ref, value, in_ref.shape[0] // GROUP, first)

    group_products(in_ref, matrix_ref, finish)


def group_fwd_kernel(in_ref, matrix_ref, out_ref):
    def finish(first, value):
        value = jnp.where(value < 0, value + MODULUS, value)
        value = jnp.where(value >= MODULUS, value - MODULUS, value)
        value = jnp.where(value < 0, value + MODULUS, value)
        scatter_rows(out_ref, value, in_ref.shape[0] // GROUP, first)

    group_products(in_ref, matrix_ref, finish)


def middle_kernel(
    in_ref,
    side_back_ref,
    mid_back_ref,
    shift_cols_ref,
    shift_rows_ref,
    own_ref,
    matrices_hbm,
    powers_hbm,
    out_ref,
    group_fwd_ref,
    long_fwd_t_ref,
    mid_fwd_ref,
    sems,
):
    wide = LIMBS * SIDE
    part = wide // SPLIT_OUT
    rows = SIDE // SPLIT_OUT
    cols = LONG // SPLIT_OUT
    copies = load(
        [
            matrices_hbm.at[pl.ds(0, 2 * wide)],
            powers_hbm.at[pl.ds(0, 2 * SIDE)],
            group_matrix(matrices_hbm, 1),
        ],
        [
            long_fwd_t_ref,
            mid_fwd_ref,
            group_fwd_ref,
        ],
        sems,
    )

    def first(k, split):
        return dot(side_back_ref[k * part : (k + 1) * part, :], split)

    def after_first(k, result):
        here = slice(k * rows, (k + 1) * rows)
        result = from_rows(result, rows)
        return digits(
            paired_mul(result, mid_back_ref[here, 0:SIDE], mid_back_ref[here, SIDE:]), 1
        )

    def second(split):
        return [
            dot(
                split,
                jnp.concatenate(
                    [
                        side_back_ref[
                            n * part + b * rows : n * part + (b + 1) * rows,
                            a * SIDE : (a + 1) * SIDE,
                        ]
                        for a in range(LIMBS)
                        for n in range(SPLIT_OUT)
                    ],
                    0,
                ),
            )
            for b in range(LIMBS)
        ]

    def after_second(k, result):
        here = slice(k * rows, (k + 1) * rows)
        result = combine(*result)
        result = paired_mul(result, shift_rows_ref[0:1, :], shift_rows_ref[8:9, :])
        lower = slice(SIDE + k * rows, SIDE + (k + 1) * rows)
        columns = [
            jnp.concatenate([shift_cols_ref[lines, :]] * (SIDE // LANES), 1)
            for lines in (here, lower)
        ]
        return digits(paired_mul(result, *columns), 1)

    ext_columns = [
        jnp.concatenate([as_column(own_ref[row : row + 1, 0:SIDE])] * (cols // LANES), 1)
        for row in (8, 9)
    ]
    split = digits(gather_rows(in_ref, SIDE, SIDE // LANES), 0)
    one = first(0, split)
    two = first(1, split)
    one = after_first(0, one)
    one = second(one)
    two = after_first(1, two)
    one = after_second(0, one)
    two = second(two)
    two = after_second(1, two)
    split = jnp.concatenate([one, two], 0)
    copies[0].wait()

    def third(k):
        return dot(split, long_fwd_t_ref[k * wide : (k + 1) * wide, :])

    def after_third(k, result):
        here = slice(k * cols, (k + 1) * cols)
        result = from_cols(result, cols)
        return digits(paired_mul(result, mid_fwd_ref[0:SIDE, here], mid_fwd_ref[SIDE:, here]), 0)

    def fourth(split):
        return dot(side_back_ref[...], split)

    def after_fourth(k, result):
        here = slice(k * cols, (k + 1) * cols)
        result = jnp.concatenate(
            [from_rows(result[n * part : (n + 1) * part], rows) for n in range(SPLIT_OUT)], 0
        )
        result = paired_mul(result, own_ref[0:1, here], own_ref[1:2, here])
        result = paired_mul(result, *ext_columns)
        scatter_rows(out_ref, result, LONG // LANES, k * cols // LANES)

    one = third(0)
    for copy in copies[1:]:
        copy.wait()
    two = third(1)
    one = fourth(after_third(0, one))
    two = after_third(1, two)
    after_fourth(0, one)
    two = fourth(two)
    after_fourth(1, two)


def limbs_kernel(in_ref, out_hbm, out_ref, sems):
    scale = np.float32(1.0 / 65536.0)
    per_line = LONG // LANES
    parts = sems.shape[0]
    rows = out_ref.shape[0] // parts
    stores = []
    for line in range(SIDE):
        value = in_ref[pl.ds(-line % SIDE * per_line, per_line), :]
        first = 2 * per_line * line
        low = (value & 65535).astype(jnp.float32) * scale
        high = (value >> 16).astype(jnp.float32) * scale
        out_ref[pl.ds(first, per_line, stride=2), :] = low
        out_ref[pl.ds(first + 1, per_line, stride=2), :] = high
        done = first + 2 * per_line
        if done % rows == 0:
            part = pl.ds(done - rows, rows)
            stores += load(
                [out_ref.at[part]], [out_hbm.at[part]], sems.at[pl.ds(len(stores), 1)]
            )
    for copy in stores:
        copy.wait()


def exchange(rows):
    blocks = rows.reshape(GROUP, rows.shape[0] // GROUP, LANES)
    moved = lax.all_to_all(blocks, "rows", split_axis=0, concat_axis=0, tiled=True)
    return moved.reshape(rows.shape)


def on_device(trace_limbs, coset_shift):
    matrices, powers = (jnp.asarray(table) for table in tables())
    place = lax.axis_index("rows").astype(jnp.int32).reshape(1)
    rows = LOCAL // LANES
    wide = LIMBS * SIDE
    smem = pl.BlockSpec(memory_space=pltpu.SMEM)
    vmem = pl.BlockSpec(memory_space=pltpu.VMEM)
    anywhere = pl.BlockSpec(memory_space=pl.ANY)

    def ints(*shape):
        return jax.ShapeDtypeStruct(shape, jnp.int32)

    def limb(*shape):
        return jax.ShapeDtypeStruct(shape, jnp.bfloat16)

    def call(
        name, body, out_shape, in_specs, scratch=(), sems=(), cost=1, out_specs=vmem, megabytes=48
    ):
        scratch = [pltpu.VMEM(a.shape, a.dtype) for a in scratch]
        scratch += [pltpu.SemaphoreType.DMA((count,)) for count in sems]
        return pl.pallas_call(
            body,
            out_shape=out_shape,
            in_specs=in_specs,
            out_specs=out_specs,
            scratch_shapes=scratch,
            compiler_params=pltpu.CompilerParams(vmem_limit_bytes=megabytes << 20),
            cost_estimate=pl.CostEstimate(
                flops=cost * 1_000_000, bytes_accessed=1 << 20, transcendentals=0
            ),
            name=name,
        )

    limbs = trace_limbs.reshape(2, rows, LANES).transpose(1, 0, 2).reshape(2 * rows, LANES)
    group_back, base, own, side_back, mid_back, shift_cols, shift_rows = call(
        "power_tables",
        tables_kernel,
        [
            limb(LIMBS * GROUP, LIMBS * GROUP),
            ints(2 * GROUP, LONG),
            ints(LINE_ROWS, LONG),
            limb(wide, wide),
            ints(SIDE, LONG),
            ints(2 * SIDE, LANES),
            ints(16, SIDE),
        ],
        [smem, smem] + [anywhere] * 2,
        [],
        (5,),
        100,
        [vmem] * 7,
    )(place, coset_shift, matrices, powers)
    values = call("join_limbs", join_kernel, ints(rows, LANES), [vmem] * 2)(limbs, shift_rows)
    columns = exchange(values)
    columns = call("group_back", group_back_kernel, ints(rows, LANES), [vmem] * 4, cost=300)(
        columns, group_back, base, own
    )
    block = exchange(columns)
    extended, group_fwd = call(
        "block_transforms",
        middle_kernel,
        [ints(2 * rows, LANES), limb(LIMBS * GROUP, LIMBS * GROUP)],
        [vmem] * 6 + [anywhere] * 2,
        [limb(2 * wide, wide), ints(2 * SIDE, LONG)],
        (3,),
        4000,
        [vmem] * 2,
    )(block, side_back, mid_back, shift_cols, shift_rows, own, matrices, powers)
    columns = exchange(extended)
    columns = call("group_fwd", group_fwd_kernel, ints(2 * rows, LANES), [vmem] * 2, cost=500)(
        columns, group_fwd
    )
    ordered = exchange(columns)
    pairs = jax.ShapeDtypeStruct((4 * rows, LANES), jnp.float32)
    pairs = call(
        "split_limbs", limbs_kernel, pairs, [vmem], [pairs], (4,), out_specs=anywhere
    )(ordered)
    return pairs.reshape(2 * rows, 2, LANES).transpose(1, 0, 2).reshape(2, 2 * rows * LANES)


def solution(mesh):
    placed = (P(None, ("cols", "rows")), P())
    return jax.shard_map(
        on_device, mesh=mesh, in_specs=placed, out_specs=P(None, ("cols", "rows")), check_vma=False
    )
```

```python
import functools

import jax
import jax.numpy as jnp
import ml_dtypes
import numpy as np
from jax import lax
from jax.experimental import pallas as pl
from jax.experimental.pallas import tpu as pltpu
from jax.sharding import PartitionSpec as P

LEN_A = 2048
LEN_B = 4096
MODULUS = 2013265921
HALF = MODULUS // 2
SPLIT = 15
LIMBS = 4
BYTE_BIAS = -2139062144

TRACE_LEN = LEN_A * LEN_B
EXT_LEN = 2 * TRACE_LEN
GROUP = 128
SIDE = 256
LONG = 2 * SIDE
LOCAL = SIDE * SIDE
LANES = 128


def unity_root(length):
    return pow(pow(31, 15, MODULUS), (1 << 27) // length, MODULUS)


BACK_ROOT = pow(unity_root(TRACE_LEN), MODULUS - 2, MODULUS)
FWD_ROOT = unity_root(EXT_LEN)


def powers_of(base, exponents):
    exponents = np.asarray(exponents, dtype=np.int64)
    result = np.ones(exponents.shape, dtype=np.int64)
    square = base % MODULUS
    for bit in range(int(exponents.max(initial=0)).bit_length()):
        result = np.where(exponents >> bit & 1 == 1, mul_mod(result, square), result)
        square = square * square % MODULUS
    return result


def mul_mod(left, right):
    return left * right % MODULUS


def centered(values):
    values = values % MODULUS
    return np.where(values > HALF, values - MODULUS, values)


def both_halves(values):
    return np.stack([centered(values), centered(mul_mod(values, 1 << SPLIT))]).astype(np.int32)


def limbs_of(values):
    rest = centered(values)
    digits = []
    for _ in range(LIMBS):
        digit = (rest + 128) % 256 - 128
        digits.append(digit)
        rest = (rest - digit) // 256
    return np.stack(digits)


def limb_matrix(matrix):
    blocks = np.stack([limbs_of(mul_mod(matrix, 256**a)) for a in range(LIMBS)], axis=2)
    out_len, in_len = matrix.shape
    return np.ascontiguousarray(
        blocks.reshape(LIMBS * out_len, LIMBS * in_len).astype(ml_dtypes.bfloat16)
    )


HALF_SIDE = SIDE // 2
MATRIX_ROWS = 4096
TABLE_ROWS = 4096
LINE_ROWS = 16
LINES_AT = 1024


@functools.cache
def tables():
    lines = np.arange(GROUP)
    side = np.arange(SIDE)
    long = np.arange(LONG)
    tile = np.arange(LOCAL // GROUP)
    half = np.arange(HALF_SIDE)
    back_side = pow(unity_root(SIDE), MODULUS - 2, MODULUS)
    root_group = unity_root(GROUP)
    back_group = pow(root_group, MODULUS - 2, MODULUS)
    back_local = pow(unity_root(LOCAL), MODULUS - 2, MODULUS)
    small = LIMBS * HALF_SIDE

    def product_matrix(root, outputs, inputs):
        return limb_matrix(powers_of(root, outputs[:, None] * inputs[None, :]))

    matrices = np.zeros((MATRIX_ROWS, 2 * small), ml_dtypes.bfloat16)
    for parity in range(2):
        long_fwd = product_matrix(unity_root(LONG), side, 2 * half + parity).T
        long_fwd = long_fwd.reshape(small, LIMBS, 2, HALF_SIDE).transpose(0, 2, 1, 3)
        matrices[parity * small : (parity + 1) * small] = long_fwd.reshape(small, 2 * small)
        matrices[2 * small : 3 * small, parity * small : (parity + 1) * small] = product_matrix(
            back_side, half, 2 * half + parity
        )
    matrices[3 * small : 4 * small, :small] = product_matrix(back_side, 2 * half + 1, half)
    matrices[3 * small : 4 * small, small:] = product_matrix(root_group, lines, lines)
    matrices[4 * small : 5 * small, :small] = product_matrix(back_group, lines, lines)

    powers = np.zeros((TABLE_ROWS, LONG), np.int32)
    powers[0:512] = both_halves(
        powers_of(unity_root(2 * LOCAL), side[:, None] * long[None, :])
    ).reshape(512, LONG)
    powers[512:768] = np.concatenate(
        both_halves(powers_of(back_local, side[:, None] * side[None, :])), axis=1
    )
    powers[768:1024] = both_halves(
        powers_of(BACK_ROOT, lines[:, None] * tile[None, :])
    ).reshape(256, LONG)
    own = np.zeros((GROUP, LINE_ROWS, LONG), np.int32)

    def place_pair(root, exponents, row, lane):
        pair = both_halves(powers_of(root, lines[:, None] * exponents[None, :]))
        own[:, row : row + 2, lane : lane + exponents.size] = pair.transpose(1, 0, 2)

    place_pair(FWD_ROOT, long, 0, 0)
    place_pair(FWD_ROOT, LONG * (-np.concatenate([2 * half, 2 * half + 1]) % SIDE), 8, 0)
    place_pair(BACK_ROOT, tile.size * lines, 8, SIDE)
    powers[LINES_AT : LINES_AT + GROUP * LINE_ROWS] = own.reshape(GROUP * LINE_ROWS, LONG)
    return matrices, powers


def toward_zero(value):
    return value.astype(jnp.int32)


def to_nearest(value):
    return jnp.floor(value + 0.5).astype(jnp.int32)


def paired_mul(value, plain, lifted, whole=toward_zero):
    high = value >> SPLIT
    low = value & ((1 << SPLIT) - 1)
    scale = np.float32(1.0 / MODULUS)
    upper = high.astype(jnp.float32) * lifted.astype(jnp.float32)
    lower = low.astype(jnp.float32) * plain.astype(jnp.float32)
    return high * lifted + low * plain - whole((upper + lower) * scale) * MODULUS


near_mul = functools.partial(paired_mul, whole=to_nearest)


def lift(value):
    once, twice = (int(centered(np.int64(1 << k * SPLIT))) for k in (1, 2))
    return near_mul(value, jnp.int32(once), jnp.int32(twice))


def digits(value, axis):
    biased = (value + jnp.int32(BYTE_BIAS)) ^ jnp.int32(BYTE_BIAS)
    parts = [(biased << (24 - 8 * k)) >> 24 for k in range(LIMBS - 1)] + [biased >> 24]
    return jnp.concatenate([part.astype(jnp.float32).astype(jnp.bfloat16) for part in parts], axis)


def combine(part0, part1, part2, part3):
    estimate = (
        part3 * np.float32(2.0**24 / MODULUS)
        + part2 * np.float32(2.0**16 / MODULUS)
        + part1 * np.float32(2.0**8 / MODULUS)
    )
    whole = [part.astype(jnp.int32) for part in (part0, part1, part2, part3)]
    total = whole[0] + (whole[1] << 8) + (whole[2] << 16) + (whole[3] << 24)
    return total - toward_zero(estimate) * MODULUS


def dot(left, right):
    return jnp.dot(left, right, preferred_element_type=jnp.float32)


def from_rows(result, count):
    return combine(*(result[k * count : (k + 1) * count] for k in range(LIMBS)))


def from_cols(result, count):
    return combine(*(result[:, k * count : (k + 1) * count] for k in range(LIMBS)))


def load(sources, targets, sems):
    copies = [
        pltpu.make_async_copy(source, target, sems.at[k])
        for k, (source, target) in enumerate(zip(sources, targets, strict=True))
    ]
    for copy in copies:
        copy.start()
    return copies


def as_column(line):
    return jnp.concatenate(
        [
            jnp.broadcast_to(line[:, k : k + LANES], (LANES, LANES)).T
            for k in range(0, line.shape[1], LANES)
        ],
        0,
    )


def own_rows(place):
    return pl.ds(pl.multiple_of(LINES_AT + place * LINE_ROWS, LINE_ROWS), LINE_ROWS)


def block_of(matrices_hbm, row, col):
    size = LIMBS * HALF_SIDE
    return matrices_hbm.at[pl.ds(row * size, size), pl.ds(col * size, size)]


def tables_kernel(
    place_ref,
    shift_ref,
    matrices_hbm,
    powers_hbm,
    group_back_ref,
    base_ref,
    own_ref,
    side_back_ref,
    mid_back_ref,
    shift_cols_ref,
    shift_rows_ref,
    sems,
):
    place = place_ref[0]
    small = LIMBS * HALF_SIDE
    copies = load(
        [
            block_of(matrices_hbm, 4, 0),
            powers_hbm.at[pl.ds(768, 2 * GROUP)],
            powers_hbm.at[own_rows(place)],
            matrices_hbm.at[pl.ds(2 * small, small)],
            powers_hbm.at[pl.ds(2 * SIDE, SIDE)],
        ],
        [group_back_ref, base_ref, own_ref, side_back_ref, mid_back_ref],
        sems,
    )

    first = jnp.full((8, LANES), shift_ref[0], jnp.int32)
    square = jnp.where(first > HALF, first - MODULUS, first)
    inverse_len = int(centered(np.int64(pow(TRACE_LEN, MODULUS - 2, MODULUS))))
    factor = jnp.full((8, LANES), inverse_len, jnp.int32)
    lines = lax.broadcasted_iota(jnp.int32, (SIDE, LANES), 0)
    column = jnp.ones((SIDE, LANES), jnp.int32)
    cols = lax.broadcasted_iota(jnp.int32, (8, SIDE), 1)
    cols = (cols & (HALF_SIDE - 1)) * 2 + (cols >> 7)
    line = None
    for bit in range(23):
        lifted = lift(square)
        if bit < 7:
            factor = jnp.where(place >> bit & 1 == 1, near_mul(factor, square, lifted), factor)
        elif bit < 15:
            plain_row, lifted_row = square[0:1], lifted[0:1]
            column = jnp.where(
                lines >> (bit - 7) & 1 == 1, near_mul(column, plain_row, lifted_row), column
            )
        else:
            if line is None:
                line = jnp.concatenate([factor] * (SIDE // LANES), 1)
            plain_row = jnp.concatenate([square] * (SIDE // LANES), 1)
            lifted_row = jnp.concatenate([lifted] * (SIDE // LANES), 1)
            line = jnp.where(
                cols >> (bit - 15) & 1 == 1, near_mul(line, plain_row, lifted_row), line
            )
        square = near_mul(square, square, lifted)
    shift_cols_ref[0:SIDE, :] = column
    shift_cols_ref[SIDE:, :] = lift(column)
    shift_rows_ref[0:8, :] = line
    shift_rows_ref[8:16, :] = lift(line)

    for copy in copies:
        copy.wait()


def join_kernel(limbs_ref, after_ref, out_ref):
    rows = out_ref.shape[0]
    low = (limbs_ref[pl.ds(0, rows, stride=2), :] * 65536.0).astype(jnp.int32)
    high = (limbs_ref[pl.ds(1, rows, stride=2), :] * 65536.0).astype(jnp.int32)
    joined = (high << 16) + low
    out_ref[...] = jnp.where(joined > HALF, joined - MODULUS, joined)


def gather_rows(ref, lines, per_line):
    return jnp.concatenate(
        [ref[pl.ds(k, lines, stride=per_line), :] for k in range(per_line)], 1
    )


def scatter_rows(ref, value, per_line, first=0):
    lines = value.shape[0]
    for k in range(value.shape[1] // LANES):
        ref[pl.ds(first + k, lines, stride=per_line), :] = value[:, k * LANES : (k + 1) * LANES]


def group_products(in_ref, matrix_ref, finish):
    per_line = in_ref.shape[0] // GROUP
    step = 2
    splits = [
        digits(
            jnp.concatenate(
                [in_ref[pl.ds(first + k, GROUP, stride=per_line), :] for k in range(step)], 1
            ),
            0,
        )
        for first in range(0, per_line, step)
    ]
    last = None
    for index, split in enumerate(splits):
        result = dot(matrix_ref[...], split)
        if last is not None:
            finish((index - 1) * step, from_rows(last, GROUP))
        last = result
    finish((len(splits) - 1) * step, from_rows(last, GROUP))


def group_back_kernel(in_ref, matrix_ref, base_ref, own_ref, out_ref):
    columns = [
        jnp.concatenate([as_column(own_ref[row : row + 1, SIDE : SIDE + LANES])] * 2, 1)
        for row in (8, 9)
    ]

    def finish(first, value):
        cols = slice(first * LANES, first * LANES + value.shape[1])
        value = paired_mul(value, base_ref[0:GROUP, cols], base_ref[GROUP:, cols])
        value = paired_mul(value, *columns)
        scatter_rows(out_ref, value, in_ref.shape[0] // GROUP, first)

    group_products(in_ref, matrix_ref, finish)


def group_fwd_kernel(in_ref, matrix_ref, out_ref):
    def finish(first, value):
        value = jnp.where(value < 0, value + MODULUS, value)
        value = jnp.where(value >= MODULUS, value - MODULUS, value)
        value = jnp.where(value < 0, value + MODULUS, value)
        scatter_rows(out_ref, value, in_ref.shape[0] // GROUP, first)

    group_products(in_ref, matrix_ref, finish)


def middle_kernel(
    in_ref,
    side_back_ref,
    mid_back_ref,
    shift_cols_ref,
    shift_rows_ref,
    own_ref,
    matrices_hbm,
    powers_hbm,
    out_ref,
    group_fwd_ref,
    long_fwd_ref,
    side_odd_ref,
    mid_fwd_ref,
    sems,
):
    small = LIMBS * HALF_SIDE
    rows = HALF_SIDE
    copies = load(
        [
            matrices_hbm.at[pl.ds(0, 2 * small)],
            powers_hbm.at[pl.ds(0, 2 * SIDE)],
            block_of(matrices_hbm, 3, 0),
            block_of(matrices_hbm, 3, 1),
        ],
        [long_fwd_ref, mid_fwd_ref, side_odd_ref, group_fwd_ref],
        sems,
    )

    def wide_columns(ref, first):
        return jnp.concatenate([ref[first : first + rows, :]] * (SIDE // LANES), 1)

    per_line = SIDE // LANES
    even, odd = (
        dot(
            side_back_ref[:, parity * small : (parity + 1) * small],
            digits(
                jnp.concatenate(
                    [
                        in_ref[pl.ds(per_line * parity + k, rows, stride=2 * per_line), :]
                        for k in range(per_line)
                    ],
                    1,
                ),
                0,
            ),
        )
        for parity in range(2)
    )

    transposed = [
        jnp.concatenate(
            [
                jnp.concatenate(
                    [
                        side_back_ref[
                            b * rows : (b + 1) * rows,
                            parity * small + a * rows : parity * small + (a + 1) * rows,
                        ]
                        for a in range(LIMBS)
                    ],
                    0,
                )
                for b in range(LIMBS)
            ],
            1,
        )
        for parity in range(2)
    ]

    def after_first(n, result):
        here = slice(n * rows, (n + 1) * rows)
        value = from_rows(result, rows)
        value = near_mul(value, mid_back_ref[here, 0:SIDE], mid_back_ref[here, SIDE:])
        left, right = value[:, 0:rows], value[:, rows:]
        return [digits(left + right, 1), digits(left - right, 1)]

    def second(splits):
        return [dot(split, matrix) for split, matrix in zip(splits, transposed, strict=True)]

    def after_second(n, results):
        splits = []
        for parity, result in enumerate(results):
            here = slice(parity * rows, (parity + 1) * rows)
            value = from_cols(result, rows)
            value = paired_mul(value, shift_rows_ref[0:1, here], shift_rows_ref[8:9, here])
            value = paired_mul(
                value,
                shift_cols_ref[n * rows : (n + 1) * rows, :],
                shift_cols_ref[SIDE + n * rows : SIDE + (n + 1) * rows, :],
            )
            splits.append(digits(value, 1))
        return splits

    one = after_first(0, even + odd)
    one = second(one)
    two = after_first(1, even - odd)
    one = after_second(0, one)
    two = second(two)
    two = after_second(1, two)
    splits = [jnp.concatenate(pair, 0) for pair in zip(one, two, strict=True)]
    copies[0].wait()

    def third(k):
        return [
            dot(
                splits[parity],
                long_fwd_ref[
                    parity * small : (parity + 1) * small, k * small : (k + 1) * small
                ],
            )
            for parity in range(2)
        ]

    def lanes_of(k):
        return [slice(k * LANES, (k + 1) * LANES), slice(SIDE + k * LANES, SIDE + (k + 1) * LANES)]

    def after_third(k, results):
        even, odd = results
        values = []
        for here, result in zip(lanes_of(k), (even + odd, even - odd), strict=True):
            value = from_cols(result, LANES)
            values.append(near_mul(value, mid_fwd_ref[0:SIDE, here], mid_fwd_ref[SIDE:, here]))
        value = jnp.concatenate(values, 1)
        upper, lower = value[0:rows], value[rows:]
        return [digits(upper + lower, 0), digits(upper - lower, 0)]

    ext_columns = [as_column(own_ref[row : row + 1, 0:SIDE]) for row in (8, 9)]

    def after_fourth(k, parity, result):
        value = from_rows(result, rows)
        plain, lifted = (
            jnp.concatenate([own_ref[row : row + 1, here] for here in lanes_of(k)], 1)
            for row in (0, 1)
        )
        value = paired_mul(value, plain, lifted)
        value = paired_mul(
            value, *(wide_columns(column, parity * rows) for column in ext_columns)
        )
        tiles = LONG // LANES
        for n, tile in enumerate((k, SIDE // LANES + k)):
            out_ref[pl.ds(parity * tiles + tile, rows, stride=2 * tiles), :] = value[
                :, n * LANES : (n + 1) * LANES
            ]

    one = third(0)
    for copy in copies[1:]:
        copy.wait()
    two = third(1)
    one = after_third(0, one)
    by_parity = [side_back_ref[:, 0:small], side_odd_ref[...]]
    one = [dot(matrix, split) for matrix, split in zip(by_parity, one, strict=True)]
    two = after_third(1, two)
    after_fourth(0, 0, one[0])
    first = dot(by_parity[0], two[0])
    after_fourth(0, 1, one[1])
    last = dot(by_parity[1], two[1])
    after_fourth(1, 0, first)
    after_fourth(1, 1, last)


def limbs_kernel(in_ref, out_hbm, out_ref, sems):
    scale = np.float32(1.0 / 65536.0)
    per_line = LONG // LANES
    parts = sems.shape[0]
    rows = out_ref.shape[0] // parts
    stores = []
    for line in range(SIDE):
        value = in_ref[pl.ds(-line % SIDE * per_line, per_line), :]
        first = 2 * per_line * line
        low = (value & 65535).astype(jnp.float32) * scale
        high = (value >> 16).astype(jnp.float32) * scale
        out_ref[pl.ds(first, per_line, stride=2), :] = low
        out_ref[pl.ds(first + 1, per_line, stride=2), :] = high
        done = first + 2 * per_line
        if done % rows == 0:
            part = pl.ds(done - rows, rows)
            stores += load(
                [out_ref.at[part]], [out_hbm.at[part]], sems.at[pl.ds(len(stores), 1)]
            )
    for copy in stores:
        copy.wait()


def exchange(rows):
    blocks = rows.reshape(GROUP, rows.shape[0] // GROUP, LANES)
    moved = lax.all_to_all(blocks, "rows", split_axis=0, concat_axis=0, tiled=True)
    return moved.reshape(rows.shape)


def on_device(trace_limbs, coset_shift):
    matrices, powers = (jnp.asarray(table) for table in tables())
    place = lax.axis_index("rows").astype(jnp.int32).reshape(1)
    rows = LOCAL // LANES
    small = LIMBS * HALF_SIDE
    smem = pl.BlockSpec(memory_space=pltpu.SMEM)
    vmem = pl.BlockSpec(memory_space=pltpu.VMEM)
    anywhere = pl.BlockSpec(memory_space=pl.ANY)

    def ints(*shape):
        return jax.ShapeDtypeStruct(shape, jnp.int32)

    def limb(*shape):
        return jax.ShapeDtypeStruct(shape, jnp.bfloat16)

    def call(
        name, body, out_shape, in_specs, scratch=(), sems=(), cost=1, out_specs=vmem, megabytes=48
    ):
        scratch = [pltpu.VMEM(a.shape, a.dtype) for a in scratch]
        scratch += [pltpu.SemaphoreType.DMA((count,)) for count in sems]
        return pl.pallas_call(
            body,
            out_shape=out_shape,
            in_specs=in_specs,
            out_specs=out_specs,
            scratch_shapes=scratch,
            compiler_params=pltpu.CompilerParams(vmem_limit_bytes=megabytes << 20),
            cost_estimate=pl.CostEstimate(
                flops=cost * 1_000_000, bytes_accessed=1 << 20, transcendentals=0
            ),
            name=name,
        )

    limbs = trace_limbs.reshape(2, rows, LANES).transpose(1, 0, 2).reshape(2 * rows, LANES)
    group_back, base, own, side_back, mid_back, shift_cols, shift_rows = call(
        "power_tables",
        tables_kernel,
        [
            limb(small, small),
            ints(2 * GROUP, LONG),
            ints(LINE_ROWS, LONG),
            limb(small, 2 * small),
            ints(SIDE, LONG),
            ints(2 * SIDE, LANES),
            ints(16, SIDE),
        ],
        [smem, smem] + [anywhere] * 2,
        [],
        (5,),
        100,
        [vmem] * 7,
    )(place, coset_shift, matrices, powers)
    values = call("join_limbs", join_kernel, ints(rows, LANES), [vmem] * 2)(limbs, shift_rows)
    columns = exchange(values)
    columns = call("group_back", group_back_kernel, ints(rows, LANES), [vmem] * 4, cost=300)(
        columns, group_back, base, own
    )
    block = exchange(columns)
    extended, group_fwd = call(
        "block_transforms",
        middle_kernel,
        [ints(2 * rows, LANES), limb(small, small)],
        [vmem] * 6 + [anywhere] * 2,
        [limb(2 * small, 2 * small), limb(small, small), ints(2 * SIDE, LONG)],
        (4,),
        4000,
        [vmem] * 2,
    )(block, side_back, mid_back, shift_cols, shift_rows, own, matrices, powers)
    columns = exchange(extended)
    columns = call("group_fwd", group_fwd_kernel, ints(2 * rows, LANES), [vmem] * 2, cost=500)(
        columns, group_fwd
    )
    ordered = exchange(columns)
    pairs = jax.ShapeDtypeStruct((4 * rows, LANES), jnp.float32)
    pairs = call(
        "split_limbs", limbs_kernel, pairs, [vmem], [pairs], (4,), out_specs=anywhere
    )(ordered)
    return pairs.reshape(2 * rows, 2, LANES).transpose(1, 0, 2).reshape(2, 2 * rows * LANES)


def solution(mesh):
    placed = (P(None, ("cols", "rows")), P())
    return jax.shard_map(
        on_device, mesh=mesh, in_specs=placed, out_specs=P(None, ("cols", "rows")), check_vma=False
    )
```

```python
import functools

import jax
import jax.numpy as jnp
import ml_dtypes
import numpy as np
from jax import lax
from jax.experimental import pallas as pl
from jax.experimental.pallas import tpu as pltpu
from jax.sharding import PartitionSpec as P

LEN_A = 2048
LEN_B = 4096
MODULUS = 2013265921
HALF = MODULUS // 2
SPLIT = 15
LIMBS = 4
BYTE_BIAS = -2139062144

TRACE_LEN = LEN_A * LEN_B
EXT_LEN = 2 * TRACE_LEN
GROUP = 128
SIDE = 256
LONG = 2 * SIDE
LOCAL = SIDE * SIDE
LANES = 128


def unity_root(length):
    return pow(pow(31, 15, MODULUS), (1 << 27) // length, MODULUS)


BACK_ROOT = pow(unity_root(TRACE_LEN), MODULUS - 2, MODULUS)
FWD_ROOT = unity_root(EXT_LEN)


def powers_of(base, exponents):
    exponents = np.asarray(exponents, dtype=np.int64)
    result = np.ones(exponents.shape, dtype=np.int64)
    square = base % MODULUS
    for bit in range(int(exponents.max(initial=0)).bit_length()):
        result = np.where(exponents >> bit & 1 == 1, mul_mod(result, square), result)
        square = square * square % MODULUS
    return result


def mul_mod(left, right):
    return left * right % MODULUS


def centered(values):
    values = values % MODULUS
    return np.where(values > HALF, values - MODULUS, values)


def both_halves(values):
    return np.stack([centered(values), centered(mul_mod(values, 1 << SPLIT))]).astype(np.int32)


def limbs_of(values):
    rest = centered(values)
    digits = []
    for _ in range(LIMBS):
        digit = (rest + 128) % 256 - 128
        digits.append(digit)
        rest = (rest - digit) // 256
    return np.stack(digits)


def limb_matrix(matrix):
    blocks = np.stack([limbs_of(mul_mod(matrix, 256**a)) for a in range(LIMBS)], axis=2)
    out_len, in_len = matrix.shape
    return np.ascontiguousarray(
        blocks.reshape(LIMBS * out_len, LIMBS * in_len).astype(ml_dtypes.bfloat16)
    )


HALF_SIDE = SIDE // 2
MATRIX_ROWS = 4096
TABLE_ROWS = 4096
LINE_ROWS = 16
LINES_AT = 1024


@functools.cache
def tables():
    lines = np.arange(GROUP)
    side = np.arange(SIDE)
    long = np.arange(LONG)
    tile = np.arange(LOCAL // GROUP)
    half = np.arange(HALF_SIDE)
    back_side = pow(unity_root(SIDE), MODULUS - 2, MODULUS)
    root_group = unity_root(GROUP)
    back_group = pow(root_group, MODULUS - 2, MODULUS)
    back_local = pow(unity_root(LOCAL), MODULUS - 2, MODULUS)
    small = LIMBS * HALF_SIDE

    def product_matrix(root, outputs, inputs):
        return limb_matrix(powers_of(root, outputs[:, None] * inputs[None, :]))

    matrices = np.zeros((MATRIX_ROWS, 2 * small), ml_dtypes.bfloat16)
    for parity in range(2):
        long_fwd = product_matrix(unity_root(LONG), side, 2 * half + parity).T
        long_fwd = long_fwd.reshape(small, LIMBS, 2, HALF_SIDE).transpose(0, 2, 1, 3)
        matrices[parity * small : (parity + 1) * small] = long_fwd.reshape(small, 2 * small)
        matrices[2 * small : 3 * small, parity * small : (parity + 1) * small] = product_matrix(
            back_side, half, 2 * half + parity
        )
    matrices[3 * small : 4 * small, :small] = product_matrix(back_side, 2 * half + 1, half)
    part = np.arange(GROUP // 2)
    for row, col, root in ((3, 1, root_group), (4, 0, back_group)):
        matrices[row * small : row * small + small // 2, col * small : (col + 1) * small] = (
            np.concatenate([product_matrix(root, part, 2 * part + k) for k in range(2)], axis=1)
        )

    powers = np.zeros((TABLE_ROWS, LONG), np.int32)
    powers[0:512] = both_halves(
        powers_of(unity_root(2 * LOCAL), side[:, None] * long[None, :])
    ).reshape(512, LONG)
    powers[512:768] = np.concatenate(
        both_halves(powers_of(back_local, side[:, None] * side[None, :])), axis=1
    )
    powers[768:1024] = both_halves(
        powers_of(BACK_ROOT, lines[:, None] * tile[None, :])
    ).reshape(256, LONG)
    own = np.zeros((GROUP, LINE_ROWS, LONG), np.int32)

    def place_pair(root, exponents, row, lane):
        pair = both_halves(powers_of(root, lines[:, None] * exponents[None, :]))
        own[:, row : row + 2, lane : lane + exponents.size] = pair.transpose(1, 0, 2)

    place_pair(FWD_ROOT, long, 0, 0)
    place_pair(FWD_ROOT, LONG * (-np.concatenate([2 * half, 2 * half + 1]) % SIDE), 8, 0)
    place_pair(BACK_ROOT, tile.size * lines, 8, SIDE)
    powers[LINES_AT : LINES_AT + GROUP * LINE_ROWS] = own.reshape(GROUP * LINE_ROWS, LONG)
    return matrices, powers


def toward_zero(value):
    return value.astype(jnp.int32)


def to_nearest(value):
    return jnp.floor(value + 0.5).astype(jnp.int32)


def paired_mul(value, plain, lifted, whole=toward_zero):
    high = value >> SPLIT
    low = value & ((1 << SPLIT) - 1)
    scale = np.float32(1.0 / MODULUS)
    upper = high.astype(jnp.float32) * lifted.astype(jnp.float32)
    lower = low.astype(jnp.float32) * plain.astype(jnp.float32)
    return high * lifted + low * plain - whole((upper + lower) * scale) * MODULUS


near_mul = functools.partial(paired_mul, whole=to_nearest)


def lift(value):
    once, twice = (int(centered(np.int64(1 << k * SPLIT))) for k in (1, 2))
    return near_mul(value, jnp.int32(once), jnp.int32(twice))


def digits(value, axis):
    biased = (value + jnp.int32(BYTE_BIAS)) ^ jnp.int32(BYTE_BIAS)
    parts = [(biased << (24 - 8 * k)) >> 24 for k in range(LIMBS - 1)] + [biased >> 24]
    return jnp.concatenate([part.astype(jnp.float32).astype(jnp.bfloat16) for part in parts], axis)


def combine(part0, part1, part2, part3):
    estimate = (
        part3 * np.float32(2.0**24 / MODULUS)
        + part2 * np.float32(2.0**16 / MODULUS)
        + part1 * np.float32(2.0**8 / MODULUS)
    )
    whole = [part.astype(jnp.int32) for part in (part0, part1, part2, part3)]
    total = whole[0] + (whole[1] << 8) + (whole[2] << 16) + (whole[3] << 24)
    return total - toward_zero(estimate) * MODULUS


def dot(left, right):
    return jnp.dot(left, right, preferred_element_type=jnp.float32)


def from_rows(result, count):
    return combine(*(result[k * count : (k + 1) * count] for k in range(LIMBS)))


def from_cols(result, count):
    return combine(*(result[:, k * count : (k + 1) * count] for k in range(LIMBS)))


def load(sources, targets, sems):
    copies = [
        pltpu.make_async_copy(source, target, sems.at[k])
        for k, (source, target) in enumerate(zip(sources, targets, strict=True))
    ]
    for copy in copies:
        copy.start()
    return copies


def as_column(line):
    return jnp.concatenate(
        [
            jnp.broadcast_to(line[:, k : k + LANES], (LANES, LANES)).T
            for k in range(0, line.shape[1], LANES)
        ],
        0,
    )


def own_rows(place):
    return pl.ds(pl.multiple_of(LINES_AT + place * LINE_ROWS, LINE_ROWS), LINE_ROWS)


def block_of(matrices_hbm, row, col, rows=LIMBS * HALF_SIDE):
    size = LIMBS * HALF_SIDE
    return matrices_hbm.at[pl.ds(row * size, rows), pl.ds(col * size, size)]


def tables_kernel(
    shift_hbm,
    matrices_hbm,
    powers_hbm,
    group_back_ref,
    base_ref,
    own_ref,
    side_back_ref,
    mid_back_ref,
    shift_cols_ref,
    shift_rows_ref,
    shift_ref,
    sems,
):
    place = lax.axis_index("rows")
    small = LIMBS * HALF_SIDE
    copies = load(
        [
            shift_hbm,
            block_of(matrices_hbm, 4, 0, LIMBS * GROUP // 2),
            powers_hbm.at[pl.ds(768, 2 * GROUP)],
            powers_hbm.at[own_rows(place)],
            matrices_hbm.at[pl.ds(2 * small, small)],
            powers_hbm.at[pl.ds(2 * SIDE, SIDE)],
        ],
        [shift_ref, group_back_ref, base_ref, own_ref, side_back_ref, mid_back_ref],
        sems,
    )
    copies[0].wait()

    first = jnp.broadcast_to(shift_ref[...], (8, LANES))
    square = jnp.where(first > HALF, first - MODULUS, first)
    inverse_len = int(centered(np.int64(pow(TRACE_LEN, MODULUS - 2, MODULUS))))
    factor = jnp.full((8, LANES), inverse_len, jnp.int32)
    lines = lax.broadcasted_iota(jnp.int32, (SIDE, LANES), 0)
    column = jnp.ones((SIDE, LANES), jnp.int32)
    cols = lax.broadcasted_iota(jnp.int32, (8, SIDE), 1)
    cols = (cols & (HALF_SIDE - 1)) * 2 + (cols >> 7)
    line = None
    for bit in range(23):
        lifted = lift(square)
        if bit < 7:
            factor = jnp.where(place >> bit & 1 == 1, near_mul(factor, square, lifted), factor)
        elif bit < 15:
            plain_row, lifted_row = square[0:1], lifted[0:1]
            column = jnp.where(
                lines >> (bit - 7) & 1 == 1, near_mul(column, plain_row, lifted_row), column
            )
        else:
            if line is None:
                line = jnp.concatenate([factor] * (SIDE // LANES), 1)
            plain_row = jnp.concatenate([square] * (SIDE // LANES), 1)
            lifted_row = jnp.concatenate([lifted] * (SIDE // LANES), 1)
            line = jnp.where(
                cols >> (bit - 15) & 1 == 1, near_mul(line, plain_row, lifted_row), line
            )
        square = near_mul(square, square, lifted)
    shift_cols_ref[0:SIDE, :] = column
    shift_cols_ref[SIDE:, :] = lift(column)
    shift_rows_ref[0:8, :] = line
    shift_rows_ref[8:16, :] = lift(line)

    for copy in copies[1:]:
        copy.wait()


def join_kernel(limbs_ref, after_ref, out_ref):
    rows = out_ref.shape[0]
    low = (limbs_ref[pl.ds(0, rows, stride=2), :] * 65536.0).astype(jnp.int32)
    high = (limbs_ref[pl.ds(1, rows, stride=2), :] * 65536.0).astype(jnp.int32)
    joined = (high << 16) + low
    out_ref[...] = jnp.where(joined > HALF, joined - MODULUS, joined)


def gather_rows(ref, lines, per_line):
    return jnp.concatenate(
        [ref[pl.ds(k, lines, stride=per_line), :] for k in range(per_line)], 1
    )


def scatter_rows(ref, value, per_line, first=0):
    lines = value.shape[0]
    for k in range(value.shape[1] // LANES):
        ref[pl.ds(first + k, lines, stride=per_line), :] = value[:, k * LANES : (k + 1) * LANES]


def group_products(in_ref, matrix_ref, finish):
    per_line = in_ref.shape[0] // GROUP
    step = 2
    half = GROUP // 2
    size = LIMBS * half

    def split(first, parity):
        lines = [
            in_ref[pl.ds(per_line * parity + first + k, half, stride=2 * per_line), :]
            for k in range(step)
        ]
        return digits(jnp.concatenate(lines, 1), 0)

    def done(first, even, odd):
        parts = [from_rows(result, half) for result in (even + odd, even - odd)]
        finish(first, jnp.concatenate(parts, 0))

    last = None
    for first in range(0, per_line, step):
        results = [
            dot(matrix_ref[:, parity * size : (parity + 1) * size], split(first, parity))
            for parity in range(2)
        ]
        if last is not None:
            done(first - step, *last)
        last = results
    done(per_line - step, *last)


def group_back_kernel(in_ref, matrix_ref, base_ref, own_ref, out_ref):
    columns = [
        jnp.concatenate([as_column(own_ref[row : row + 1, SIDE : SIDE + LANES])] * 2, 1)
        for row in (8, 9)
    ]

    def finish(first, value):
        cols = slice(first * LANES, first * LANES + value.shape[1])
        value = paired_mul(value, base_ref[0:GROUP, cols], base_ref[GROUP:, cols])
        value = paired_mul(value, *columns)
        scatter_rows(out_ref, value, in_ref.shape[0] // GROUP, first)

    group_products(in_ref, matrix_ref, finish)


def group_fwd_kernel(in_ref, matrix_ref, out_ref):
    def finish(first, value):
        value = jnp.where(value < 0, value + MODULUS, value)
        value = jnp.where(value >= MODULUS, value - MODULUS, value)
        value = jnp.where(value < 0, value + MODULUS, value)
        scatter_rows(out_ref, value, in_ref.shape[0] // GROUP, first)

    group_products(in_ref, matrix_ref, finish)


def middle_kernel(
    in_ref,
    side_back_ref,
    mid_back_ref,
    shift_cols_ref,
    shift_rows_ref,
    own_ref,
    matrices_hbm,
    powers_hbm,
    out_ref,
    group_fwd_ref,
    long_fwd_ref,
    side_odd_ref,
    mid_fwd_ref,
    sems,
):
    small = LIMBS * HALF_SIDE
    rows = HALF_SIDE
    copies = load(
        [
            matrices_hbm.at[pl.ds(0, 2 * small)],
            powers_hbm.at[pl.ds(0, 2 * SIDE)],
            block_of(matrices_hbm, 3, 0),
            block_of(matrices_hbm, 3, 1, LIMBS * GROUP // 2),
        ],
        [long_fwd_ref, mid_fwd_ref, side_odd_ref, group_fwd_ref],
        sems,
    )

    def wide_columns(ref, first):
        return jnp.concatenate([ref[first : first + rows, :]] * (SIDE // LANES), 1)

    per_line = SIDE // LANES
    even, odd = (
        dot(
            side_back_ref[:, parity * small : (parity + 1) * small],
            digits(
                jnp.concatenate(
                    [
                        in_ref[pl.ds(per_line * parity + k, rows, stride=2 * per_line), :]
                        for k in range(per_line)
                    ],
                    1,
                ),
                0,
            ),
        )
        for parity in range(2)
    )

    transposed = [
        jnp.concatenate(
            [
                jnp.concatenate(
                    [
                        side_back_ref[
                            b * rows : (b + 1) * rows,
                            parity * small + a * rows : parity * small + (a + 1) * rows,
                        ]
                        for a in range(LIMBS)
                    ],
                    0,
                )
                for b in range(LIMBS)
            ],
            1,
        )
        for parity in range(2)
    ]

    def after_first(n, result):
        here = slice(n * rows, (n + 1) * rows)
        value = from_rows(result, rows)
        value = near_mul(value, mid_back_ref[here, 0:SIDE], mid_back_ref[here, SIDE:])
        left, right = value[:, 0:rows], value[:, rows:]
        return [digits(left + right, 1), digits(left - right, 1)]

    def second(splits):
        return [dot(split, matrix) for split, matrix in zip(splits, transposed, strict=True)]

    def after_second(n, results):
        splits = []
        for parity, result in enumerate(results):
            here = slice(parity * rows, (parity + 1) * rows)
            value = from_cols(result, rows)
            value = paired_mul(value, shift_rows_ref[0:1, here], shift_rows_ref[8:9, here])
            value = paired_mul(
                value,
                shift_cols_ref[n * rows : (n + 1) * rows, :],
                shift_cols_ref[SIDE + n * rows : SIDE + (n + 1) * rows, :],
            )
            splits.append(digits(value, 1))
        return splits

    one = after_first(0, even + odd)
    one = second(one)
    two = after_first(1, even - odd)
    one = after_second(0, one)
    two = second(two)
    two = after_second(1, two)
    splits = [jnp.concatenate(pair, 0) for pair in zip(one, two, strict=True)]
    copies[0].wait()

    def third(k):
        return [
            dot(
                splits[parity],
                long_fwd_ref[
                    parity * small : (parity + 1) * small, k * small : (k + 1) * small
                ],
            )
            for parity in range(2)
        ]

    def lanes_of(k):
        return [slice(k * LANES, (k + 1) * LANES), slice(SIDE + k * LANES, SIDE + (k + 1) * LANES)]

    def after_third(k, results):
        even, odd = results
        values = []
        for here, result in zip(lanes_of(k), (even + odd, even - odd), strict=True):
            value = from_cols(result, LANES)
            values.append(near_mul(value, mid_fwd_ref[0:SIDE, here], mid_fwd_ref[SIDE:, here]))
        value = jnp.concatenate(values, 1)
        upper, lower = value[0:rows], value[rows:]
        return [digits(upper + lower, 0), digits(upper - lower, 0)]

    ext_columns = [as_column(own_ref[row : row + 1, 0:SIDE]) for row in (8, 9)]

    def after_fourth(k, parity, result):
        value = from_rows(result, rows)
        plain, lifted = (
            jnp.concatenate([own_ref[row : row + 1, here] for here in lanes_of(k)], 1)
            for row in (0, 1)
        )
        value = paired_mul(value, plain, lifted)
        value = paired_mul(
            value, *(wide_columns(column, parity * rows) for column in ext_columns)
        )
        tiles = LONG // LANES
        for n, tile in enumerate((k, SIDE // LANES + k)):
            out_ref[pl.ds(parity * tiles + tile, rows, stride=2 * tiles), :] = value[
                :, n * LANES : (n + 1) * LANES
            ]

    one = third(0)
    for copy in copies[1:]:
        copy.wait()
    two = third(1)
    one = after_third(0, one)
    by_parity = [side_back_ref[:, 0:small], side_odd_ref[...]]
    one = [dot(matrix, split) for matrix, split in zip(by_parity, one, strict=True)]
    two = after_third(1, two)
    after_fourth(0, 0, one[0])
    first = dot(by_parity[0], two[0])
    after_fourth(0, 1, one[1])
    last = dot(by_parity[1], two[1])
    after_fourth(1, 0, first)
    after_fourth(1, 1, last)


def limbs_kernel(in_ref, out_hbm, out_ref, sems):
    scale = np.float32(1.0 / 65536.0)
    per_line = LONG // LANES
    parts = sems.shape[0]
    rows = out_ref.shape[0] // parts
    stores = []
    for line in range(SIDE):
        value = in_ref[pl.ds(-line % SIDE * per_line, per_line), :]
        first = 2 * per_line * line
        low = (value & 65535).astype(jnp.float32) * scale
        high = (value >> 16).astype(jnp.float32) * scale
        out_ref[pl.ds(first, per_line, stride=2), :] = low
        out_ref[pl.ds(first + 1, per_line, stride=2), :] = high
        done = first + 2 * per_line
        if done % rows == 0:
            part = pl.ds(done - rows, rows)
            stores += load(
                [out_ref.at[part]], [out_hbm.at[part]], sems.at[pl.ds(len(stores), 1)]
            )
    for copy in stores:
        copy.wait()


def exchange(rows):
    blocks = rows.reshape(GROUP, rows.shape[0] // GROUP, LANES)
    moved = lax.all_to_all(blocks, "rows", split_axis=0, concat_axis=0, tiled=True)
    return moved.reshape(rows.shape)


def on_device(trace_limbs, coset_shift):
    matrices, powers = (jnp.asarray(table) for table in tables())
    rows = LOCAL // LANES
    small = LIMBS * HALF_SIDE
    smem = pl.BlockSpec(memory_space=pltpu.SMEM)
    vmem = pl.BlockSpec(memory_space=pltpu.VMEM)
    anywhere = pl.BlockSpec(memory_space=pl.ANY)

    def ints(*shape):
        return jax.ShapeDtypeStruct(shape, jnp.int32)

    def limb(*shape):
        return jax.ShapeDtypeStruct(shape, jnp.bfloat16)

    def call(
        name, body, out_shape, in_specs, scratch=(), sems=(), cost=1, out_specs=vmem, megabytes=48
    ):
        scratch = [pltpu.VMEM(a.shape, a.dtype) for a in scratch]
        scratch += [pltpu.SemaphoreType.DMA((count,)) for count in sems]
        return pl.pallas_call(
            body,
            out_shape=out_shape,
            in_specs=in_specs,
            out_specs=out_specs,
            scratch_shapes=scratch,
            compiler_params=pltpu.CompilerParams(vmem_limit_bytes=megabytes << 20),
            cost_estimate=pl.CostEstimate(
                flops=cost * 1_000_000, bytes_accessed=1 << 20, transcendentals=0
            ),
            name=name,
        )

    limbs = trace_limbs.reshape(2, rows, LANES).transpose(1, 0, 2).reshape(2 * rows, LANES)
    group_back, base, own, side_back, mid_back, shift_cols, shift_rows = call(
        "power_tables",
        tables_kernel,
        [
            limb(small // 2, small),
            ints(2 * GROUP, LONG),
            ints(LINE_ROWS, LONG),
            limb(small, 2 * small),
            ints(SIDE, LONG),
            ints(2 * SIDE, LANES),
            ints(16, SIDE),
        ],
        [anywhere] * 3,
        [ints(1, 1)],
        (6,),
        100,
        [vmem] * 7,
    )(coset_shift.reshape(1, 1), matrices, powers)
    values = call("join_limbs", join_kernel, ints(rows, LANES), [vmem] * 2)(limbs, shift_rows)
    columns = exchange(values)
    columns = call("group_back", group_back_kernel, ints(rows, LANES), [vmem] * 4, cost=300)(
        columns, group_back, base, own
    )
    block = exchange(columns)
    extended, group_fwd = call(
        "block_transforms",
        middle_kernel,
        [ints(2 * rows, LANES), limb(small // 2, small)],
        [vmem] * 6 + [anywhere] * 2,
        [limb(2 * small, 2 * small), limb(small, small), ints(2 * SIDE, LONG)],
        (4,),
        4000,
        [vmem] * 2,
    )(block, side_back, mid_back, shift_cols, shift_rows, own, matrices, powers)
    columns = exchange(extended)
    columns = call("group_fwd", group_fwd_kernel, ints(2 * rows, LANES), [vmem] * 2, cost=500)(
        columns, group_fwd
    )
    ordered = exchange(columns)
    pairs = jax.ShapeDtypeStruct((4 * rows, LANES), jnp.float32)
    pairs = call(
        "split_limbs", limbs_kernel, pairs, [vmem], [pairs], (4,), out_specs=anywhere
    )(ordered)
    return pairs.reshape(2 * rows, 2, LANES).transpose(1, 0, 2).reshape(2, 2 * rows * LANES)


def solution(mesh):
    placed = (P(None, ("cols", "rows")), P())
    return jax.shard_map(
        on_device, mesh=mesh, in_specs=placed, out_specs=P(None, ("cols", "rows")), check_vma=False
    )
```

```python
import functools

import jax
import jax.numpy as jnp
import ml_dtypes
import numpy as np
from jax import lax
from jax.experimental import pallas as pl
from jax.experimental.pallas import tpu as pltpu
from jax.sharding import PartitionSpec as P

LEN_A = 2048
LEN_B = 4096
MODULUS = 2013265921
HALF = MODULUS // 2
SPLIT = 15
LIMBS = 4
BYTE_BIAS = -2139062144

TRACE_LEN = LEN_A * LEN_B
EXT_LEN = 2 * TRACE_LEN
GROUP = 128
SIDE = 256
LONG = 2 * SIDE
LOCAL = SIDE * SIDE
LANES = 128


def unity_root(length):
    return pow(pow(31, 15, MODULUS), (1 << 27) // length, MODULUS)


BACK_ROOT = pow(unity_root(TRACE_LEN), MODULUS - 2, MODULUS)
FWD_ROOT = unity_root(EXT_LEN)


def powers_of(base, exponents):
    exponents = np.asarray(exponents, dtype=np.int64)
    result = np.ones(exponents.shape, dtype=np.int64)
    square = base % MODULUS
    for bit in range(int(exponents.max(initial=0)).bit_length()):
        result = np.where(exponents >> bit & 1 == 1, mul_mod(result, square), result)
        square = square * square % MODULUS
    return result


def mul_mod(left, right):
    return left * right % MODULUS


def centered(values):
    values = values % MODULUS
    return np.where(values > HALF, values - MODULUS, values)


def both_halves(values):
    return np.stack([centered(values), centered(mul_mod(values, 1 << SPLIT))]).astype(np.int32)


def limbs_of(values):
    rest = centered(values)
    digits = []
    for _ in range(LIMBS):
        digit = (rest + 128) % 256 - 128
        digits.append(digit)
        rest = (rest - digit) // 256
    return np.stack(digits)


def limb_matrix(matrix):
    blocks = np.stack([limbs_of(mul_mod(matrix, 256**a)) for a in range(LIMBS)], axis=2)
    out_len, in_len = matrix.shape
    return np.ascontiguousarray(
        blocks.reshape(LIMBS * out_len, LIMBS * in_len).astype(ml_dtypes.bfloat16)
    )


HALF_SIDE = SIDE // 2
MATRIX_ROWS = 4096
TABLE_ROWS = 4096
LINE_ROWS = 16
LINES_AT = 1024


@functools.cache
def tables():
    lines = np.arange(GROUP)
    side = np.arange(SIDE)
    long = np.arange(LONG)
    tile = np.arange(LOCAL // GROUP)
    half = np.arange(HALF_SIDE)
    back_side = pow(unity_root(SIDE), MODULUS - 2, MODULUS)
    root_group = unity_root(GROUP)
    back_group = pow(root_group, MODULUS - 2, MODULUS)
    back_local = pow(unity_root(LOCAL), MODULUS - 2, MODULUS)
    small = LIMBS * HALF_SIDE

    def product_matrix(root, outputs, inputs):
        return limb_matrix(powers_of(root, outputs[:, None] * inputs[None, :]))

    matrices = np.zeros((MATRIX_ROWS, 2 * small), ml_dtypes.bfloat16)
    for parity in range(2):
        long_fwd = product_matrix(unity_root(LONG), side, 2 * half + parity).T
        long_fwd = long_fwd.reshape(small, LIMBS, 2, HALF_SIDE).transpose(0, 2, 1, 3)
        matrices[parity * small : (parity + 1) * small] = long_fwd.reshape(small, 2 * small)
        matrices[2 * small : 3 * small, parity * small : (parity + 1) * small] = product_matrix(
            back_side, half, 2 * half + parity
        )
    matrices[3 * small : 4 * small, :small] = product_matrix(back_side, 2 * half + 1, half)
    part = np.arange(GROUP // 2)
    for row, col, root in ((3, 1, root_group), (4, 0, back_group)):
        matrices[row * small : row * small + small // 2, col * small : (col + 1) * small] = (
            np.concatenate([product_matrix(root, part, 2 * part + k) for k in range(2)], axis=1)
        )

    powers = np.zeros((TABLE_ROWS, LONG), np.int32)
    powers[0:512] = both_halves(
        powers_of(unity_root(2 * LOCAL), side[:, None] * long[None, :])
    ).reshape(512, LONG)
    powers[512:768] = np.concatenate(
        both_halves(powers_of(back_local, side[:, None] * side[None, :])), axis=1
    )
    powers[768:1024] = both_halves(
        powers_of(BACK_ROOT, lines[:, None] * tile[None, :])
    ).reshape(256, LONG)
    own = np.zeros((GROUP, LINE_ROWS, LONG), np.int32)

    def place_pair(root, exponents, row, lane):
        pair = both_halves(powers_of(root, lines[:, None] * exponents[None, :]))
        own[:, row : row + 2, lane : lane + exponents.size] = pair.transpose(1, 0, 2)

    place_pair(FWD_ROOT, long, 0, 0)
    place_pair(FWD_ROOT, LONG * (-np.concatenate([2 * half, 2 * half + 1]) % SIDE), 8, 0)
    place_pair(BACK_ROOT, tile.size * lines, 8, SIDE)
    powers[LINES_AT : LINES_AT + GROUP * LINE_ROWS] = own.reshape(GROUP * LINE_ROWS, LONG)
    return matrices, powers


def toward_zero(value):
    return value.astype(jnp.int32)


def to_nearest(value):
    return jnp.floor(value + 0.5).astype(jnp.int32)


def paired_mul(value, plain, lifted, whole=toward_zero):
    high = value >> SPLIT
    low = value & ((1 << SPLIT) - 1)
    scale = np.float32(1.0 / MODULUS)
    upper = high.astype(jnp.float32) * lifted.astype(jnp.float32)
    lower = low.astype(jnp.float32) * plain.astype(jnp.float32)
    return high * lifted + low * plain - whole((upper + lower) * scale) * MODULUS


near_mul = functools.partial(paired_mul, whole=to_nearest)


def lift(value):
    once, twice = (int(centered(np.int64(1 << k * SPLIT))) for k in (1, 2))
    return near_mul(value, jnp.int32(once), jnp.int32(twice))


def digits(value, axis):
    biased = (value + jnp.int32(BYTE_BIAS)) ^ jnp.int32(BYTE_BIAS)
    parts = [(biased << (24 - 8 * k)) >> 24 for k in range(LIMBS - 1)] + [biased >> 24]
    return jnp.concatenate([part.astype(jnp.float32).astype(jnp.bfloat16) for part in parts], axis)


def combine(part0, part1, part2, part3, whole_of=toward_zero):
    estimate = (
        part3 * np.float32(2.0**24 / MODULUS)
        + part2 * np.float32(2.0**16 / MODULUS)
        + part1 * np.float32(2.0**8 / MODULUS)
    )
    whole = [part.astype(jnp.int32) for part in (part0, part1, part2, part3)]
    total = whole[0] + (whole[1] << 8) + (whole[2] << 16) + (whole[3] << 24)
    return total - whole_of(estimate) * MODULUS


def dot(left, right):
    return jnp.dot(left, right, preferred_element_type=jnp.float32)


def from_rows(result, count, whole_of=toward_zero):
    return combine(*(result[k * count : (k + 1) * count] for k in range(LIMBS)), whole_of=whole_of)


def from_cols(result, count):
    return combine(*(result[:, k * count : (k + 1) * count] for k in range(LIMBS)))


def load(sources, targets, sems):
    copies = [
        pltpu.make_async_copy(source, target, sems.at[k])
        for k, (source, target) in enumerate(zip(sources, targets, strict=True))
    ]
    for copy in copies:
        copy.start()
    return copies


def as_column(line):
    return jnp.concatenate(
        [
            jnp.broadcast_to(line[:, k : k + LANES], (LANES, LANES)).T
            for k in range(0, line.shape[1], LANES)
        ],
        0,
    )


def own_rows(place):
    return pl.ds(pl.multiple_of(LINES_AT + place * LINE_ROWS, LINE_ROWS), LINE_ROWS)


def block_of(matrices_hbm, row, col, rows=LIMBS * HALF_SIDE):
    size = LIMBS * HALF_SIDE
    return matrices_hbm.at[pl.ds(row * size, rows), pl.ds(col * size, size)]


def tables_kernel(
    shift_hbm,
    matrices_hbm,
    powers_hbm,
    group_back_ref,
    base_ref,
    own_ref,
    side_back_ref,
    mid_back_ref,
    shift_cols_ref,
    shift_rows_ref,
    shift_ref,
    sems,
):
    place = lax.axis_index("rows")
    small = LIMBS * HALF_SIDE
    copies = load(
        [
            shift_hbm,
            block_of(matrices_hbm, 4, 0, LIMBS * GROUP // 2),
            powers_hbm.at[pl.ds(768, 2 * GROUP)],
            powers_hbm.at[own_rows(place)],
            matrices_hbm.at[pl.ds(2 * small, small)],
            powers_hbm.at[pl.ds(2 * SIDE, SIDE)],
        ],
        [shift_ref, group_back_ref, base_ref, own_ref, side_back_ref, mid_back_ref],
        sems,
    )
    copies[0].wait()

    first = jnp.broadcast_to(shift_ref[...], (8, LANES))
    square = jnp.where(first > HALF, first - MODULUS, first)
    inverse_len = int(centered(np.int64(pow(TRACE_LEN, MODULUS - 2, MODULUS))))
    factor = jnp.full((8, LANES), inverse_len, jnp.int32)
    lines = lax.broadcasted_iota(jnp.int32, (SIDE, LANES), 0)
    column = jnp.ones((SIDE, LANES), jnp.int32)
    cols = lax.broadcasted_iota(jnp.int32, (8, SIDE), 1)
    cols = (cols & (HALF_SIDE - 1)) * 2 + (cols >> 7)
    line = None
    for bit in range(23):
        lifted = lift(square)
        if bit < 7:
            factor = jnp.where(place >> bit & 1 == 1, near_mul(factor, square, lifted), factor)
        elif bit < 15:
            plain_row, lifted_row = square[0:1], lifted[0:1]
            column = jnp.where(
                lines >> (bit - 7) & 1 == 1, near_mul(column, plain_row, lifted_row), column
            )
        else:
            if line is None:
                line = jnp.concatenate([factor] * (SIDE // LANES), 1)
            plain_row = jnp.concatenate([square] * (SIDE // LANES), 1)
            lifted_row = jnp.concatenate([lifted] * (SIDE // LANES), 1)
            line = jnp.where(
                cols >> (bit - 15) & 1 == 1, near_mul(line, plain_row, lifted_row), line
            )
        square = near_mul(square, square, lifted)
    shift_cols_ref[0:SIDE, :] = column
    shift_cols_ref[SIDE:, :] = lift(column)
    shift_rows_ref[0:8, :] = line
    shift_rows_ref[8:16, :] = lift(line)

    for copy in copies[1:]:
        copy.wait()


def join_kernel(limbs_ref, after_ref, out_ref):
    rows = out_ref.shape[0]
    low = (limbs_ref[pl.ds(0, rows, stride=2), :] * 65536.0).astype(jnp.int32)
    high = (limbs_ref[pl.ds(1, rows, stride=2), :] * 65536.0).astype(jnp.int32)
    joined = (high << 16) + low
    out_ref[...] = jnp.where(joined > HALF, joined - MODULUS, joined)


def gather_rows(ref, lines, per_line):
    return jnp.concatenate(
        [ref[pl.ds(k, lines, stride=per_line), :] for k in range(per_line)], 1
    )


def scatter_rows(ref, value, per_line, first=0):
    lines = value.shape[0]
    for k in range(value.shape[1] // LANES):
        ref[pl.ds(first + k, lines, stride=per_line), :] = value[:, k * LANES : (k + 1) * LANES]


def group_products(in_ref, matrix_ref, finish, whole_of=toward_zero):
    per_line = in_ref.shape[0] // GROUP
    step = 2
    half = GROUP // 2
    size = LIMBS * half

    def split(first, parity):
        lines = [
            in_ref[pl.ds(per_line * parity + first + k, half, stride=2 * per_line), :]
            for k in range(step)
        ]
        return digits(jnp.concatenate(lines, 1), 0)

    def done(first, even, odd):
        parts = [from_rows(result, half, whole_of) for result in (even + odd, even - odd)]
        finish(first, jnp.concatenate(parts, 0))

    last = None
    for first in range(0, per_line, step):
        results = [
            dot(matrix_ref[:, parity * size : (parity + 1) * size], split(first, parity))
            for parity in range(2)
        ]
        if last is not None:
            done(first - step, *last)
        last = results
    done(per_line - step, *last)


def group_back_kernel(in_ref, matrix_ref, base_ref, own_ref, out_ref):
    columns = [
        jnp.concatenate([as_column(own_ref[row : row + 1, SIDE : SIDE + LANES])] * 2, 1)
        for row in (8, 9)
    ]

    def finish(first, value):
        cols = slice(first * LANES, first * LANES + value.shape[1])
        value = paired_mul(value, base_ref[0:GROUP, cols], base_ref[GROUP:, cols])
        value = paired_mul(value, *columns)
        scatter_rows(out_ref, value, in_ref.shape[0] // GROUP, first)

    group_products(in_ref, matrix_ref, finish)


def group_fwd_kernel(in_ref, matrix_ref, out_ref):
    def finish(first, value):
        value = jnp.where(value < 0, value + MODULUS, value)
        scatter_rows(out_ref, value, in_ref.shape[0] // GROUP, first)

    group_products(in_ref, matrix_ref, finish, to_nearest)


def middle_kernel(
    in_ref,
    side_back_ref,
    mid_back_ref,
    shift_cols_ref,
    shift_rows_ref,
    own_ref,
    matrices_hbm,
    powers_hbm,
    out_ref,
    group_fwd_ref,
    long_fwd_ref,
    side_odd_ref,
    mid_fwd_ref,
    sems,
):
    small = LIMBS * HALF_SIDE
    rows = HALF_SIDE
    copies = load(
        [
            matrices_hbm.at[pl.ds(0, 2 * small)],
            powers_hbm.at[pl.ds(0, 2 * SIDE)],
            block_of(matrices_hbm, 3, 0),
            block_of(matrices_hbm, 3, 1, LIMBS * GROUP // 2),
        ],
        [long_fwd_ref, mid_fwd_ref, side_odd_ref, group_fwd_ref],
        sems,
    )

    def wide_columns(ref, first):
        return jnp.concatenate([ref[first : first + rows, :]] * (SIDE // LANES), 1)

    per_line = SIDE // LANES
    even, odd = (
        dot(
            side_back_ref[:, parity * small : (parity + 1) * small],
            digits(
                jnp.concatenate(
                    [
                        in_ref[pl.ds(per_line * parity + k, rows, stride=2 * per_line), :]
                        for k in range(per_line)
                    ],
                    1,
                ),
                0,
            ),
        )
        for parity in range(2)
    )

    transposed = [
        jnp.concatenate(
            [
                jnp.concatenate(
                    [
                        side_back_ref[
                            b * rows : (b + 1) * rows,
                            parity * small + a * rows : parity * small + (a + 1) * rows,
                        ]
                        for a in range(LIMBS)
                    ],
                    0,
                )
                for b in range(LIMBS)
            ],
            1,
        )
        for parity in range(2)
    ]

    def after_first(n, result):
        here = slice(n * rows, (n + 1) * rows)
        value = from_rows(result, rows)
        value = near_mul(value, mid_back_ref[here, 0:SIDE], mid_back_ref[here, SIDE:])
        left, right = value[:, 0:rows], value[:, rows:]
        return [digits(left + right, 1), digits(left - right, 1)]

    def second(splits):
        return [dot(split, matrix) for split, matrix in zip(splits, transposed, strict=True)]

    def after_second(n, results):
        splits = []
        for parity, result in enumerate(results):
            here = slice(parity * rows, (parity + 1) * rows)
            value = from_cols(result, rows)
            value = paired_mul(value, shift_rows_ref[0:1, here], shift_rows_ref[8:9, here])
            value = paired_mul(
                value,
                shift_cols_ref[n * rows : (n + 1) * rows, :],
                shift_cols_ref[SIDE + n * rows : SIDE + (n + 1) * rows, :],
            )
            splits.append(digits(value, 1))
        return splits

    one = after_first(0, even + odd)
    one = second(one)
    two = after_first(1, even - odd)
    one = after_second(0, one)
    two = second(two)
    two = after_second(1, two)
    splits = [jnp.concatenate(pair, 0) for pair in zip(one, two, strict=True)]
    copies[0].wait()

    def third(k):
        return [
            dot(
                splits[parity],
                long_fwd_ref[
                    parity * small : (parity + 1) * small, k * small : (k + 1) * small
                ],
            )
            for parity in range(2)
        ]

    def lanes_of(k):
        return [slice(k * LANES, (k + 1) * LANES), slice(SIDE + k * LANES, SIDE + (k + 1) * LANES)]

    def after_third(k, results):
        even, odd = results
        values = []
        for here, result in zip(lanes_of(k), (even + odd, even - odd), strict=True):
            value = from_cols(result, LANES)
            values.append(near_mul(value, mid_fwd_ref[0:SIDE, here], mid_fwd_ref[SIDE:, here]))
        value = jnp.concatenate(values, 1)
        upper, lower = value[0:rows], value[rows:]
        return [digits(upper + lower, 0), digits(upper - lower, 0)]

    ext_columns = [as_column(own_ref[row : row + 1, 0:SIDE]) for row in (8, 9)]

    def after_fourth(k, parity, result):
        value = from_rows(result, rows)
        plain, lifted = (
            jnp.concatenate([own_ref[row : row + 1, here] for here in lanes_of(k)], 1)
            for row in (0, 1)
        )
        value = paired_mul(value, plain, lifted)
        value = paired_mul(
            value, *(wide_columns(column, parity * rows) for column in ext_columns)
        )
        tiles = LONG // LANES
        for n, tile in enumerate((k, SIDE // LANES + k)):
            out_ref[pl.ds(parity * tiles + tile, rows, stride=2 * tiles), :] = value[
                :, n * LANES : (n + 1) * LANES
            ]

    one = third(0)
    for copy in copies[1:]:
        copy.wait()
    two = third(1)
    one = after_third(0, one)
    by_parity = [side_back_ref[:, 0:small], side_odd_ref[...]]
    one = [dot(matrix, split) for matrix, split in zip(by_parity, one, strict=True)]
    two = after_third(1, two)
    after_fourth(0, 0, one[0])
    first = dot(by_parity[0], two[0])
    after_fourth(0, 1, one[1])
    last = dot(by_parity[1], two[1])
    after_fourth(1, 0, first)
    after_fourth(1, 1, last)


def limbs_kernel(in_ref, out_hbm, out_ref, sems):
    scale = np.float32(1.0 / 65536.0)
    per_line = LONG // LANES
    parts = sems.shape[0]
    rows = out_ref.shape[0] // parts
    stores = []
    for line in range(SIDE):
        value = in_ref[pl.ds(-line % SIDE * per_line, per_line), :]
        first = 2 * per_line * line
        low = (value & 65535).astype(jnp.float32) * scale
        high = (value >> 16).astype(jnp.float32) * scale
        out_ref[pl.ds(first, per_line, stride=2), :] = low
        out_ref[pl.ds(first + 1, per_line, stride=2), :] = high
        done = first + 2 * per_line
        if done % rows == 0:
            part = pl.ds(done - rows, rows)
            stores += load(
                [out_ref.at[part]], [out_hbm.at[part]], sems.at[pl.ds(len(stores), 1)]
            )
    for copy in stores:
        copy.wait()


def exchange(rows):
    blocks = rows.reshape(GROUP, rows.shape[0] // GROUP, LANES)
    moved = lax.all_to_all(blocks, "rows", split_axis=0, concat_axis=0, tiled=True)
    return moved.reshape(rows.shape)


def on_device(trace_limbs, coset_shift):
    matrices, powers = (jnp.asarray(table) for table in tables())
    rows = LOCAL // LANES
    small = LIMBS * HALF_SIDE
    smem = pl.BlockSpec(memory_space=pltpu.SMEM)
    vmem = pl.BlockSpec(memory_space=pltpu.VMEM)
    anywhere = pl.BlockSpec(memory_space=pl.ANY)

    def ints(*shape):
        return jax.ShapeDtypeStruct(shape, jnp.int32)

    def limb(*shape):
        return jax.ShapeDtypeStruct(shape, jnp.bfloat16)

    def call(
        name, body, out_shape, in_specs, scratch=(), sems=(), cost=1, out_specs=vmem, megabytes=48
    ):
        scratch = [pltpu.VMEM(a.shape, a.dtype) for a in scratch]
        scratch += [pltpu.SemaphoreType.DMA((count,)) for count in sems]
        return pl.pallas_call(
            body,
            out_shape=out_shape,
            in_specs=in_specs,
            out_specs=out_specs,
            scratch_shapes=scratch,
            compiler_params=pltpu.CompilerParams(vmem_limit_bytes=megabytes << 20),
            cost_estimate=pl.CostEstimate(
                flops=cost * 1_000_000, bytes_accessed=1 << 20, transcendentals=0
            ),
            name=name,
        )

    limbs = trace_limbs.reshape(2, rows, LANES).transpose(1, 0, 2).reshape(2 * rows, LANES)
    group_back, base, own, side_back, mid_back, shift_cols, shift_rows = call(
        "power_tables",
        tables_kernel,
        [
            limb(small // 2, small),
            ints(2 * GROUP, LONG),
            ints(LINE_ROWS, LONG),
            limb(small, 2 * small),
            ints(SIDE, LONG),
            ints(2 * SIDE, LANES),
            ints(16, SIDE),
        ],
        [anywhere] * 3,
        [ints(1, 1)],
        (6,),
        100,
        [vmem] * 7,
    )(coset_shift.reshape(1, 1), matrices, powers)
    values = call("join_limbs", join_kernel, ints(rows, LANES), [vmem] * 2)(limbs, shift_rows)
    columns = exchange(values)
    columns = call("group_back", group_back_kernel, ints(rows, LANES), [vmem] * 4, cost=300)(
        columns, group_back, base, own
    )
    block = exchange(columns)
    extended, group_fwd = call(
        "block_transforms",
        middle_kernel,
        [ints(2 * rows, LANES), limb(small // 2, small)],
        [vmem] * 6 + [anywhere] * 2,
        [limb(2 * small, 2 * small), limb(small, small), ints(2 * SIDE, LONG)],
        (4,),
        4000,
        [vmem] * 2,
    )(block, side_back, mid_back, shift_cols, shift_rows, own, matrices, powers)
    columns = exchange(extended)
    columns = call("group_fwd", group_fwd_kernel, ints(2 * rows, LANES), [vmem] * 2, cost=500)(
        columns, group_fwd
    )
    ordered = exchange(columns)
    pairs = jax.ShapeDtypeStruct((4 * rows, LANES), jnp.float32)
    pairs = call(
        "split_limbs", limbs_kernel, pairs, [vmem], [pairs], (4,), out_specs=anywhere
    )(ordered)
    return pairs.reshape(2 * rows, 2, LANES).transpose(1, 0, 2).reshape(2, 2 * rows * LANES)


def solution(mesh):
    placed = (P(None, ("cols", "rows")), P())
    return jax.shard_map(
        on_device, mesh=mesh, in_specs=placed, out_specs=P(None, ("cols", "rows")), check_vma=False
    )
```
